256 devices in a mesh: seq: 32 (over y_lo, z, core), head: 8 (over x, y_hi).
Axes of the slice: x: 4, y: 4 (y_hi: 2, y_lo: 2; y = y_hi * 2 + y_lo), z: 8, core: 2. Of those that a mesh axis runs over, the one named last changes fastest.
Arguments:
- queries: bfloat16 [12288, 5120], P('seq', 'head'), may hold values from -256 to 256
- keys: bfloat16 [12288, 5120], P('seq', 'head'), may hold values from -10 to 10
- values: bfloat16 [12288, 5120], P('seq', 'head'), may hold values from -18 to 18
- ref_keys: bfloat16 [1536, 5120], P('seq', 'head'), may hold values from -9 to 9
- ref_values: bfloat16 [1536, 5120], P('seq', 'head'), may hold values from -18 to 18
- out_weight: bfloat16 [5120, 5120], P('head'), may hold values from -0.078125 to 0.078125
Outputs:
- projected: bfloat16 [12288, 5120], P('seq', 'head')
The draws below stay inside these ranges and needn't reach their ends.
All inputs are finite; a program needn't handle non-finite values.
Results may differ from the reference program's by a relative error of at most 0.018.
Values may be sent and summed in bfloat16 or wider, within the bound.
No kernel may reach another device: no remote copies, remote signals or barrier semaphores. Data moves between devices by JAX's collectives and lax.ppermute only.
A program may use at most 128 MiB of HBM per device.

```python
import jax
import jax.numpy as jnp
from jax import lax

D = 5120
HD = 128
HEADS = 40
FRAMES = 8
FRAME_LEN = 1536
TOKENS = 12288
REF = 1536


def shared_rows(key):
    base = 1.5 * jax.random.normal(key, (TOKENS, HEADS * HD), jnp.float32)
    return jnp.clip(base, -9.0, 9.0)


def draw_keys(key, part):
    base = shared_rows(key)
    return base.astype(jnp.bfloat16)


def draw_queries(key, part):
    key = jax.random.fold_in(key, 7)
    fresh = jnp.clip(1.5 * jax.random.normal(key, (TOKENS, HEADS * HD), jnp.float32), -9.0, 9.0)
    return fresh.astype(jnp.bfloat16)


def level_of(rng, shape, shards, low, top_value):
    gain = 1.0
    for position, parts in shards:
        heights = jax.random.uniform(jax.random.fold_in(jax.random.fold_in(rng, 6), position), (parts,), jnp.float32, low / len(shards), top_value / len(shards))
        gain = gain * jnp.repeat(jnp.exp(heights), shape[position] // parts).reshape((-1,) + (1,) * (len(shape) - 1 - position))
    return gain


def noise(rng, extent, spread, bound, split=(), dtype=jnp.bfloat16):
    factor_of = level_of(rng, extent, split, -0.22, 0.18) if split else 1.0
    entries = jax.random.normal(rng, extent, jnp.float32) * spread * factor_of
    return jnp.minimum(jnp.maximum(entries, -bound), bound).astype(dtype)


def setup_inputs(seed: int = 0) -> dict:
    arg_keys = jax.random.split(jax.random.key(seed), 7)
    return {
        "queries": draw_queries(jax.random.fold_in(arg_keys[6], 71), 0),
        "keys": draw_keys(jax.random.fold_in(arg_keys[6], 71), 0),
        "values": noise(arg_keys[2], (TOKENS, HEADS * HD), 3.0, 18.0, ((0, 32), (1, 8))),
        "ref_keys": noise(arg_keys[3], (REF, HEADS * HD), 1.5, 9.0, ((0, 32), (1, 8))),
        "ref_values": noise(arg_keys[4], (REF, HEADS * HD), 3.0, 18.0, ((0, 32), (1, 8))),
        "out_weight": noise(arg_keys[5], (HEADS * HD, D), (HEADS * HD) ** -0.5, 0.078125, ((0, 8),)),
    }


def attend_head(operands):
    query_rows, key_rows, value_rows = operands
    scores = jnp.dot(query_rows, key_rows.T, preferred_element_type=jnp.float32) * (1.0 / HD ** 0.5)
    peak = jnp.max(scores, axis=1, keepdims=True)
    weights = jnp.exp(scores - peak)
    total = jnp.sum(weights, axis=1, keepdims=True)
    summed = jnp.dot(weights.astype(jnp.bfloat16), value_rows, preferred_element_type=jnp.float32)
    return (summed / total).astype(jnp.bfloat16)


def reference(queries, keys, values, ref_keys, ref_values, out_weight):
    frame_queries = queries.reshape(FRAMES, FRAME_LEN, HEADS, HD)
    frame_keys = keys.reshape(FRAMES, FRAME_LEN, HEADS, HD)
    frame_values = values.reshape(FRAMES, FRAME_LEN, HEADS, HD)
    shared_keys = ref_keys.reshape(REF, HEADS, HD)
    shared_values = ref_values.reshape(REF, HEADS, HD)

    def one_frame(operands):
        query_part, key_part, value_part = operands
        all_keys = jnp.concatenate([key_part, shared_keys], axis=0)
        all_values = jnp.concatenate([value_part, shared_values], axis=0)
        per_head = lax.map(attend_head, (query_part.transpose(1, 0, 2), all_keys.transpose(1, 0, 2), all_values.transpose(1, 0, 2)))
        return per_head.transpose(1, 0, 2).reshape(FRAME_LEN, HEADS * HD)

    attended = lax.map(one_frame, (frame_queries, frame_keys, frame_values)).reshape(TOKENS, HEADS * HD)
    return jnp.dot(attended, out_weight, preferred_element_type=jnp.float32).astype(jnp.bfloat16)
```

```python
import functools
import math

import jax
import jax.numpy as jnp
from jax import lax
from jax.experimental import pallas as pl
from jax.experimental.pallas import tpu as pltpu
from jax.sharding import PartitionSpec as P

HD = 128
Z = 8
X = 4
BASE2 = math.log2(math.e) / math.sqrt(HD)
F32 = jnp.float32
BF16 = jnp.bfloat16
VMEM_LIMIT = 48 << 20


def seq_place(i):
    return i // (2 * Z), (i // 2) % Z, i % 2


def along_z(step):
    pairs = []
    for i in range(4 * Z):
        y, z, core = seq_place(i)
        pairs.append((i, (y * Z + (z + step) % Z) * 2 + core))
    return pairs


def between_frames():
    pairs = []
    for i in range(4 * Z):
        y, z, core = seq_place(i)
        other = (z + 1) % Z if z % 2 else (z - 1) % Z
        pairs.append((i, (y * Z + other) * 2 + core))
    return pairs


def along_x(step):
    return [(i, (i // 2 + step) % X * 2 + i % 2) for i in range(2 * X)]


def swap(value, axis, bit):
    return lax.ppermute(value, axis, [(i, i ^ bit) for i in range(lax.axis_size(axis))])


def scores_of(rows, keys):
    return lax.dot_general(rows, keys, (((1,), (1,)), ((), ())), preferred_element_type=F32)


def softmax_part(rows, keys, values_and_ones):
    scores = scores_of(rows, keys)
    peak = jnp.max(scores, axis=1, keepdims=True)
    weights = jnp.exp2((scores - peak) * BASE2).astype(BF16)
    both = jnp.dot(weights, values_and_ones, preferred_element_type=F32)
    return both[:, :HD], both[:, HD:], peak * BASE2


def fill_keys(key_ref, value_ref, layout, pieces):
    at = 0
    for piece, kind in zip(pieces, layout):
        if kind[0] == "key":
            key_ref[at : at + kind[1], :] = piece[...]
        elif kind[0] == "value":
            value_ref[at : at + kind[1], :HD] = piece[...]
            at += kind[1]
        else:
            half = kind[1]
            for group in range(kind[2]):
                low = group * 2 * half
                key_ref[at : at + half, :] = piece[low : low + half, :]
                value_ref[at : at + half, :HD] = piece[low + half : low + 2 * half, :]
                at += half
    value_ref[:, HD:] = jnp.ones((at, HD), BF16)


def first_kernel(layout, *refs):
    queries = refs[:2]
    pieces = refs[2 : 2 + len(layout)]
    part_ref, log_ref, key_ref, value_ref = refs[2 + len(layout) :]
    fill_keys(key_ref, value_ref, layout, pieces)
    rows = queries[0].shape[0]
    for place, query in enumerate(queries):
        summed, total, peak = softmax_part(query[...], key_ref[...], value_ref[...])
        part_ref[place * rows : (place + 1) * rows, :] = summed / total
        log_ref[place * rows : (place + 1) * rows, :] = peak + jnp.log2(total)


def last_kernel(layout, low, high, *refs):
    queries = refs[:2]
    states = refs[2:6]
    pieces = refs[6 : 6 + len(layout)]
    own_ref, own_log, other_ref, other_log, key_ref, value_ref, query_ref = refs[6 + len(layout) :]
    rows = high - low
    head = pl.program_id(0)
    fill_keys(key_ref, value_ref, layout, pieces)
    query_ref[:rows, :] = queries[0][low:high, :]
    query_ref[rows:, :] = queries[1][low:high, :]
    summed, total, peak = softmax_part(query_ref[...], key_ref[...], value_ref[...])
    lane = lax.broadcasted_iota(jnp.int32, (rows, HD), 1)
    for place, (out_ref, log_ref) in enumerate(((own_ref, own_log), (other_ref, other_log))):
        part = slice(place * rows, (place + 1) * rows)
        before = states[2 * place][low:high, :]
        before_log = states[2 * place + 1][low:high, :]
        top = jnp.maximum(before_log, peak[part])
        before_factor = jnp.exp2(before_log - top)
        factor = jnp.exp2(peak[part] - top)
        whole = before_factor + total[part] * factor
        out_ref[...] = ((before * before_factor + summed[part] * factor) / whole).astype(BF16)
        logs = top + jnp.log2(whole)
        log_ref[...] = jnp.where(lane == head, logs, jnp.where(head == 0, 0.0, log_ref[...]))


def piece_keys(layout):
    return sum(
        kind[1] if kind[0] == "value" else kind[1] * kind[2] if kind[0] == "both" else 0
        for kind in layout
    )


def by_head(array, place=0, rows=None):
    return pl.BlockSpec((rows or array.shape[0], HD), lambda head: (place, head))


def estimate(rows, keys, heads):
    return pl.CostEstimate(
        flops=4 * rows * keys * heads * HD,
        bytes_accessed=4 * (rows + keys) * heads * HD,
        transcendentals=rows * keys * heads,
    )


def attend_first(queries, other_queries, layout, pieces):
    rows, width = queries.shape
    heads = width // HD
    keys = piece_keys(layout)
    shape = jax.ShapeDtypeStruct((2 * rows, width), F32)
    return pl.pallas_call(
        functools.partial(first_kernel, layout),
        grid=(heads,),
        in_specs=[by_head(a) for a in (queries, other_queries, *pieces)],
        out_specs=[by_head(shape)] * 2,
        out_shape=[shape] * 2,
        scratch_shapes=[pltpu.VMEM((keys, HD), BF16), pltpu.VMEM((keys, 2 * HD), BF16)],
        compiler_params=pltpu.CompilerParams(vmem_limit_bytes=VMEM_LIMIT),
        cost_estimate=estimate(2 * rows, keys, heads),
        name="attend_first",
    )(queries, other_queries, *pieces)


def attend_last(queries, other_queries, state, low, high, layout, pieces):
    width = queries.shape[1]
    heads = width // HD
    keys = piece_keys(layout)
    rows = high - low
    whole = queries.shape[0]
    part = jax.ShapeDtypeStruct((rows, width), BF16)
    logs = jax.ShapeDtypeStruct((rows, HD), F32)
    one = pl.BlockSpec((rows, HD), lambda head: (0, 0))
    return pl.pallas_call(
        functools.partial(last_kernel, layout, low, high),
        grid=(heads,),
        in_specs=[by_head(queries), by_head(other_queries)]
        + [by_head(a, place, whole) for place in range(2) for a in state]
        + [by_head(a) for a in pieces],
        out_specs=[by_head(part), one, by_head(part), one],
        out_shape=[part, logs, part, logs],
        scratch_shapes=[
            pltpu.VMEM((keys, HD), BF16),
            pltpu.VMEM((keys, 2 * HD), BF16),
            pltpu.VMEM((2 * rows, HD), BF16),
        ],
        compiler_params=pltpu.CompilerParams(vmem_limit_bytes=VMEM_LIMIT),
        cost_estimate=estimate(2 * rows, keys, heads),
        name="attend_last",
    )(queries, other_queries, *state, *state, *pieces)


def merge_heads(parts, logs, out_ref):
    for head in range(out_ref.shape[1] // HD):
        columns = slice(head * HD, (head + 1) * HD)
        first, second = (log[:, head : head + 1] for log in logs)
        top = jnp.maximum(first, second)
        first_factor = jnp.exp2(first - top)
        second_factor = jnp.exp2(second - top)
        scale = 1.0 / (first_factor + second_factor)
        out_ref[:, columns] = (
            parts[0][:, columns].astype(F32) * (first_factor * scale)
            + parts[1][:, columns].astype(F32) * (second_factor * scale)
        ).astype(BF16)


def send_kernel(steps, blocks_of, cols, own, own_log, got, got_log, weight, *out):
    outs, att = out[:-1], out[-1]
    step = pl.program_id(0)

    @pl.when(step == 0)
    def _():
        merge_heads((own, got), (own_log, got_log), att)

    result = jnp.dot(att[...], weight[...], preferred_element_type=F32).astype(BF16)
    for number, out_ref in enumerate(outs):

        @pl.when(step // blocks_of == number)
        def _():
            out_ref[...] = result


def project_send(cols, own, own_log, got, got_log, out_weight, n_outs):
    rows, width = own.shape
    blocks = cols.shape[0]
    blocks_of = blocks // n_outs

    def place(number):
        def index(step, cols):
            return (jnp.clip(step - number * blocks_of, 0, blocks_of - 1), 0)

        return index

    def whole(a):
        return pl.BlockSpec(a.shape, lambda step, cols: (0, 0))

    return pl.pallas_call(
        functools.partial(send_kernel, blocks, blocks_of),
        grid_spec=pltpu.PrefetchScalarGridSpec(
            num_scalar_prefetch=1,
            grid=(blocks,),
            in_specs=[whole(a) for a in (own, own_log, got, got_log)]
            + [pl.BlockSpec((width, width), lambda step, cols: (0, cols[step]))],
            out_specs=[pl.BlockSpec((rows, width), place(n)) for n in range(n_outs)]
            + [pl.BlockSpec((rows, width), lambda step, cols: (0, 0))],
        ),
        out_shape=[jax.ShapeDtypeStruct((blocks_of * rows, width), BF16)] * n_outs
        + [jax.ShapeDtypeStruct((rows, width), BF16)],
        compiler_params=pltpu.CompilerParams(vmem_limit_bytes=VMEM_LIMIT),
        cost_estimate=pl.CostEstimate(
            flops=2 * rows * width * width * blocks,
            bytes_accessed=2 * width * width * blocks,
            transcendentals=0,
        ),
        name="project_send",
    )(cols, own, own_log, got, got_log, out_weight)


def keep_kernel(cols, att, weight, out):
    out[...] = jnp.dot(att[...], weight[...], preferred_element_type=F32)


def project_keep(cols, att, out_weight):
    rows, width = att.shape
    blocks = cols.shape[0]
    return pl.pallas_call(
        keep_kernel,
        grid_spec=pltpu.PrefetchScalarGridSpec(
            num_scalar_prefetch=1,
            grid=(blocks,),
            in_specs=[
                pl.BlockSpec((rows, width), lambda step, cols: (0, 0)),
                pl.BlockSpec((width, width), lambda step, cols: (0, cols[step])),
            ],
            out_specs=pl.BlockSpec((rows, width), lambda step, cols: (step, 0)),
        ),
        out_shape=jax.ShapeDtypeStruct((blocks * rows, width), F32),
        compiler_params=pltpu.CompilerParams(vmem_limit_bytes=VMEM_LIMIT),
        cost_estimate=pl.CostEstimate(
            flops=2 * rows * width * width * blocks,
            bytes_accessed=2 * width * width * blocks,
            transcendentals=0,
        ),
        name="project_keep",
    )(cols, att, out_weight)


def added(kept, *got):
    total = kept
    for part in got:
        total = total + part.astype(F32)
    return total


def body(queries, keys, values, ref_keys, ref_values, out_weight):
    rows = queries.shape[0]
    half = ref_keys.shape[0]
    right_z, left_z, between = along_z(1), along_z(-1), between_frames()
    right_x, left_x = along_x(1), along_x(-1)
    odd = (lax.axis_index("seq") // 2) % 2 == 1

    own = jnp.concatenate([ref_keys, ref_values], axis=0)
    from_left = [lax.ppermute(own, "seq", right_z)]
    from_right = [lax.ppermute(own, "seq", left_z)]
    other_queries = swap(queries, "seq", 1)
    frame_keys = swap(keys, "seq", 2)
    frame_values = swap(values, "seq", 2)
    across = []
    for step in range(2):
        packed = [from_left[-1], from_right[-1]]
        if step == 0:
            packed = [own, *packed]
        from_left.append(lax.ppermute(from_left[-1], "seq", right_z))
        from_right.append(lax.ppermute(from_right[-1], "seq", left_z))
        across.append(swap(jnp.concatenate(packed, axis=0), "seq", 2 * Z))
    far = lax.ppermute(jnp.where(odd, from_left[-1], from_right[-1]), "seq", between)
    across.append(swap(jnp.concatenate([from_left[-1], from_right[-1]], axis=0), "seq", 2 * Z))
    across.append(swap(far, "seq", 2 * Z))

    first_layout = (("key", rows), ("value", rows))
    state = attend_first(queries, other_queries, first_layout, (keys, values))
    pieces = [frame_keys, frame_values]
    layout = [("key", rows), ("value", rows)]
    for piece in (own, *from_left, *from_right, far, *across):
        pieces.append(piece)
        layout.append(("both", half, piece.shape[0] // (2 * half)))
    layout = tuple(layout)

    cut = rows // 2
    place = lax.axis_index("head")
    mine, theirs = place % 2, 1 - place % 2
    ahead = [(place // 2 + step) % X * 2 for step in (2, 1, X - 1, 0)]

    def columns(*which):
        return jnp.stack([ahead[n] + side for n, side in which]).astype(jnp.int32)

    def finish(low, high):
        own_part, own_log, other_part, other_log = attend_last(
            queries, other_queries, state, low, high, layout, pieces
        )
        return own_part, own_log, swap(other_part, "seq", 1), swap(other_log, "seq", 1)

    n = cut
    done = finish(0, cut)
    go_right, go_left, att = project_send(
        columns((0, mine), (1, theirs), (0, theirs), (2, mine)), *done, out_weight, 2
    )
    got_left = lax.ppermute(go_right, "head", right_x)
    got_right = lax.ppermute(go_left, "head", left_x)

    m = rows - cut
    last_done = finish(cut, rows)
    go_across, last_att = project_send(
        columns(*((n, theirs) for n in range(4))), *last_done, out_weight, 1
    )
    got_across = swap(go_across, "head", 1)

    kept = project_keep(columns((1, mine), (2, theirs), (0 + 3, mine), (3, theirs)), att, out_weight)
    last_kept = project_keep(columns(*((n, mine) for n in range(4))), last_att, out_weight)

    on_right = lax.ppermute(added(kept[:n], got_left[:n]).astype(BF16), "head", right_x)
    on_left = lax.ppermute(added(kept[n : 2 * n], got_right[:n]).astype(BF16), "head", left_x)

    quarter = m // 2
    summed = [added(last_kept[k * m : (k + 1) * m], got_across[k * m : (k + 1) * m]) for k in range(4)]
    last_right = jnp.concatenate([summed[0][:quarter], summed[1][quarter:]], axis=0).astype(BF16)
    last_left = jnp.concatenate([summed[0][quarter:], summed[2][:quarter]], axis=0).astype(BF16)
    last_got_left = lax.ppermute(last_right, "head", right_x)
    last_got_right = lax.ppermute(last_left, "head", left_x)

    theirs_sum = added(kept[3 * n :], on_left, got_left[n:]).astype(BF16)
    mine_got = swap(theirs_sum, "head", 1)
    mine_sum = added(kept[2 * n : 3 * n], on_right, got_right[n:])

    last_on_right = lax.ppermute(
        added(summed[1][:quarter], last_got_left[:quarter]).astype(BF16), "head", right_x
    )
    last_on_left = lax.ppermute(
        added(summed[2][quarter:], last_got_right[:quarter]).astype(BF16), "head", left_x
    )
    return jnp.concatenate(
        [
            added(mine_sum, mine_got),
            added(summed[3][:quarter], last_on_right, last_got_right[quarter:]),
            added(summed[3][quarter:], last_on_left, last_got_left[quarter:]),
        ],
        axis=0,
    ).astype(BF16)


def solution(mesh):
    placed = (
        P("seq", "head"),
        P("seq", "head"),
        P("seq", "head"),
        P("seq", "head"),
        P("seq", "head"),
        P("head", None),
    )
    return jax.shard_map(
        body, mesh=mesh, in_specs=placed, out_specs=P("seq", "head"), check_vma=False
    )
```

```python
import functools
import math

import jax
import jax.numpy as jnp
from jax import lax
from jax.experimental import pallas as pl
from jax.experimental.pallas import tpu as pltpu
from jax.sharding import PartitionSpec as P

HD = 128
Z = 8
X = 4
BASE2 = math.log2(math.e) / math.sqrt(HD)
F32 = jnp.float32
BF16 = jnp.bfloat16
VMEM_LIMIT = 20 << 20
IN_VMEM = pl.BlockSpec(memory_space=pltpu.VMEM)
CUT = 224
CHUNKS = 4
LITTLE = pl.CostEstimate(flops=1, bytes_accessed=1, transcendentals=0)


def seq_place(i):
    return i // (2 * Z), (i // 2) % Z, i % 2


def between_frames():
    pairs = []
    for i in range(4 * Z):
        y, z, core = seq_place(i)
        other = (z + 1) % Z if z % 2 else (z - 1) % Z
        pairs.append((i, (y * Z + other) * 2 + core))
    return pairs


def along_x(step):
    return [(i, (i // 2 + step) % X * 2 + i % 2) for i in range(2 * X)]


def swap(value, axis, bit):
    return lax.ppermute(value, axis, [(i, i ^ bit) for i in range(lax.axis_size(axis))])


def held(array):
    return pltpu.with_memory_space_constraint(array, pltpu.VMEM)


def local(kernel, outs, *ins, scalars=(), scratch=(), name="local"):
    return pl.pallas_call(
        kernel,
        in_specs=[pl.BlockSpec(memory_space=pltpu.SMEM)] * len(scalars) + [IN_VMEM] * len(ins),
        out_specs=[IN_VMEM] * len(outs),
        out_shape=[pltpu.VMEM(shape, dtype) for shape, dtype in outs],
        scratch_shapes=list(scratch),
        compiler_params=pltpu.CompilerParams(vmem_limit_bytes=VMEM_LIMIT),
        cost_estimate=LITTLE,
        name=name,
    )(*scalars, *(held(a) for a in ins))


def stack_kernel(parts, *refs):
    ins, out, sems = refs[:-2], refs[-2], refs[-1]
    copies = []
    at = 0
    for number, (place, low, high) in enumerate(parts):
        rows = high - low
        copies.append(
            pltpu.make_async_copy(
                ins[place].at[low:high, :], out.at[at : at + rows, :], sems.at[number]
            )
        )
        at += rows
    for copy in copies:
        copy.start()
    for copy in copies:
        copy.wait()


def stacked(*arrays, parts=None):
    parts = parts or tuple((n, 0, a.shape[0]) for n, a in enumerate(arrays))
    rows = sum(high - low for _, low, high in parts)
    return pl.pallas_call(
        functools.partial(stack_kernel, parts),
        in_specs=[pl.BlockSpec(memory_space=pl.ANY)] * len(arrays),
        out_specs=IN_VMEM,
        out_shape=pltpu.VMEM((rows, arrays[0].shape[1]), arrays[0].dtype),
        scratch_shapes=[pltpu.SemaphoreType.DMA((len(parts),))],
        compiler_params=pltpu.CompilerParams(vmem_limit_bytes=VMEM_LIMIT),
        cost_estimate=LITTLE,
        name="stacked",
    )(*arrays)


def scores_of(rows, keys):
    return lax.dot_general(rows, keys, (((1,), (1,)), ((), ())), preferred_element_type=F32)


def fill_keys(key_ref, value_ref, halves, pieces, columns):
    at = 0
    for half, piece in zip(halves, pieces):
        for low in range(0, piece.shape[0], 2 * half):
            key_ref[at : at + half, :] = piece[low : low + half, columns]
            value_ref[at : at + half, :HD] = piece[low + half : low + 2 * half, columns]
            at += half
    value_ref[:, HD:] = jnp.ones((at, HD), BF16)


def attend_kernel(halves, low, high, with_state, last, *refs):
    queries, refs = refs[:2], refs[2:]
    if with_state:
        (before, before_log), refs = refs[:2], refs[2:]
    pieces, refs = refs[: len(halves)], refs[len(halves) :]
    if last:
        (own_ref, own_log, other_ref, key_ref, value_ref, query_ref, log_ref) = refs
    else:
        (part_ref, log_ref, key_ref, value_ref, query_ref) = refs
    rows = high - low
    whole_rows = queries[0].shape[0]
    heads = queries[0].shape[1] // HD
    for head in range(heads):
        columns = slice(head * HD, (head + 1) * HD)
        slot = head % 2
        fill_keys(key_ref.at[slot], value_ref.at[slot], halves, pieces, columns)
        for place in range(2):
            query_ref[slot, place * rows : (place + 1) * rows, :] = queries[place][low:high, columns]
        scores = scores_of(query_ref[slot], key_ref[slot])
        peak = jnp.max(scores, axis=1, keepdims=True)
        weights = jnp.exp2((scores - peak) * BASE2).astype(BF16)
        both = jnp.dot(weights, value_ref[slot], preferred_element_type=F32)
        summed, total = both[:, :HD], both[:, HD:]
        peak = peak * BASE2
        for place in range(2):
            part = slice(place * rows, (place + 1) * rows)
            if with_state:
                held_rows = slice(place * whole_rows + low, place * whole_rows + high)
                log = before_log[held_rows, head : head + 1]
                top = jnp.maximum(log, peak[part])
                before_factor = jnp.exp2(log - top)
                factor = jnp.exp2(peak[part] - top)
                whole = before_factor + total[part] * factor
                result = (before[held_rows, columns] * before_factor + summed[part] * factor) / whole
            else:
                top = peak[part]
                whole = total[part]
                result = summed[part] / whole
            if last:
                (own_ref, other_ref)[place][:, columns] = result.astype(BF16)
            else:
                part_ref[part, columns] = result
            log_ref[part, head : head + 1] = (top + jnp.log2(whole))[:, :1]
    if last:
        lane = lax.broadcasted_iota(jnp.int32, (rows, HD), 1)
        own_log[...] = log_ref[:rows, :]
        logs = log_ref[rows:, :]
        high_part = logs.astype(BF16).astype(F32)
        rest = logs - high_part
        middle = rest.astype(BF16).astype(F32)
        packed = jnp.where(
            lane < 8,
            high_part,
            jnp.where(lane < 16, pltpu.roll(middle, 8, 1), pltpu.roll(rest - middle, 16, 1)),
        )
        other_ref[:, heads * HD :] = jnp.where(lane < 24, packed, 0.0).astype(BF16)


def attend(queries, other_queries, low, high, halves, pieces, state=None, last=False):
    whole_rows, width = queries.shape
    heads = width // HD
    rows = high - low
    keys = sum(piece.shape[0] for piece in pieces) // 2
    if last:
        outs = [((rows, width), BF16), ((rows, HD), F32), ((rows, width + HD), BF16)]
    else:
        outs = [((2 * rows, width), F32), ((2 * rows, HD), F32)]
    return local(
        functools.partial(attend_kernel, halves, low, high, state is not None, last),
        outs,
        queries,
        other_queries,
        *(state or ()),
        *pieces,
        scratch=[
            pltpu.VMEM((2, keys, HD), BF16),
            pltpu.VMEM((2, keys, 2 * HD), BF16),
            pltpu.VMEM((2, 2 * rows, HD), BF16),
        ]
        + [pltpu.VMEM((2 * rows, HD), F32)] * last,
        name="attend_last" if last else "attend_part",
    )


def merge_heads(own, own_log, got, att):
    width = own.shape[1]
    logs = got[:, width:].astype(F32)
    got_log = logs + pltpu.roll(logs, HD - 8, 1) + pltpu.roll(logs, HD - 16, 1)
    for head in range(width // HD):
        columns = slice(head * HD, (head + 1) * HD)
        first, second = own_log[:, head : head + 1], got_log[:, head : head + 1]
        top = jnp.maximum(first, second)
        first_factor = jnp.exp2(first - top)
        second_factor = jnp.exp2(second - top)
        scale = 1.0 / (first_factor + second_factor)
        att[:, columns] = (
            own[:, columns].astype(F32) * (first_factor * scale)
            + got[:, columns].astype(F32) * (second_factor * scale)
        ).astype(BF16)


def products(blocks, place, att, weight, outs):
    rows, width = att.shape
    number = 0
    x, side = place[0] // 2, place[0] % 2
    for out in outs:
        for low in range(0, out.shape[0], rows):
            step, flip = blocks[number]
            block = lax.rem(x + step, X) * 2 + (1 - side if flip else side)
            at = pl.multiple_of(block * width, HD)
            result = jnp.dot(att[...], weight[:, pl.ds(at, width)], preferred_element_type=F32)
            out[low : low + rows, :] = result.astype(out.dtype)
            number += 1


def send_kernel(blocks, place, own, own_log, got, weight, *outs):
    merge_heads(own, own_log, got, outs[-1])
    products(blocks, place, outs[-1], weight, outs[:-1])


def project_send(blocks, place, own, own_log, got, weight, n_outs):
    rows, width = own.shape
    count = len(blocks)
    outs = [((count // n_outs * rows, width), BF16)] * n_outs + [((rows, width), BF16)]
    return local(
        functools.partial(send_kernel, blocks),
        outs,
        own,
        own_log,
        got,
        weight,
        scalars=(place,),
        name="project_send",
    )


def keep_kernel(blocks, place, att, weight, out):
    products(blocks, place, att, weight, (out,))


def project_keep(blocks, place, att, weight):
    rows, width = att.shape
    count = len(blocks)
    return local(
        functools.partial(keep_kernel, blocks),
        [((count * rows, width), F32)],
        att,
        weight,
        scalars=(place,),
        name="project_keep",
    )[0]


def relay_kernel(kept, got_left, got_right, to_right, to_left):
    n = to_right.shape[0]
    to_right[...] = (kept[:n, :] + got_left[:n, :].astype(F32)).astype(BF16)
    to_left[...] = (kept[n : 2 * n, :] + got_right[:n, :].astype(F32)).astype(BF16)


def turn_kernel(kept, got_left, on_left, out):
    n = out.shape[0]
    out[...] = (
        kept[3 * n :, :] + on_left[...].astype(F32) + got_left[n:, :].astype(F32)
    ).astype(BF16)


def spread_kernel(kept, got, to_right, to_left, rest):
    m = to_right.shape[0]
    q = m // 2

    def total(block, low, high):
        rows = slice(block * m + low, block * m + high)
        return kept[rows, :] + got[rows, :].astype(F32)

    to_right[:q, :] = total(0, 0, q).astype(BF16)
    to_right[q:, :] = total(1, q, m).astype(BF16)
    to_left[:q, :] = total(0, q, m).astype(BF16)
    to_left[q:, :] = total(2, 0, q).astype(BF16)
    rest[:q, :] = total(1, 0, q)
    rest[q:m, :] = total(2, q, m)
    rest[m:, :] = total(3, 0, m)


def last_kernel(kept, on_right, got_right, mine, rest, on_right2, on_left2, left2, right2, out):
    n = on_right.shape[0]
    m = left2.shape[0]
    q = m // 2
    out[:n, :] = (
        kept[2 * n : 3 * n, :]
        + on_right[...].astype(F32)
        + got_right[n:, :].astype(F32)
        + mine[...].astype(F32)
    ).astype(BF16)
    out[n : n + q, :] = (
        rest[m : m + q, :] + on_right2[...].astype(F32) + right2[q:, :].astype(F32)
    ).astype(BF16)
    out[n + q :, :] = (
        rest[m + q :, :] + on_left2[...].astype(F32) + left2[q:, :].astype(F32)
    ).astype(BF16)


def body(queries, keys, values, ref_keys, ref_values, out_weight):
    rows, width = queries.shape
    half = ref_keys.shape[0]
    between = between_frames()
    right_x, left_x = along_x(1), along_x(-1)
    place = lax.axis_index("head").reshape(1)
    place, ref_keys = lax.optimization_barrier((place, ref_keys))

    own = stacked(ref_keys, ref_values)
    inner = [swap(own, "seq", 2)]
    outer = [lax.ppermute(own, "seq", between)]
    other_queries = swap(queries, "seq", 1)
    frame, other_frame, across = [], [], []

    def exchange_chunk(number, after):
        part = rows // CHUNKS
        low, high = number * part, (number + 1) * part
        held_back, _ = lax.optimization_barrier(((keys, values), after))
        chunk = stacked(*held_back, parts=((0, low, high), (1, low, high)))
        frame.append(chunk)
        other_frame.append(swap(chunk, "seq", 2))

    exchange_chunk(0, other_queries)
    for step in range(3):
        came_inner, came_outer = inner[-1], outer[-1]
        if step < 2:
            inner.append(swap(came_outer, "seq", 2))
        outer.append(lax.ppermute(came_inner, "seq", between))
        packed = stacked(*([own] * (step == 0)), came_inner, came_outer)
        exchange_chunk(step + 1, packed)
        across.append(swap(packed, "seq", 2 * Z))
    far, frame, other_frame = lax.optimization_barrier((outer[-1], frame, other_frame))
    across.append(swap(far, "seq", 2 * Z))
    state = attend(
        queries, other_queries, 0, rows, (rows // CHUNKS,) * (2 * CHUNKS), (*frame, *other_frame)
    )
    pieces = (own, *inner, *outer[:-1], far, *across)
    halves = (half,) * len(pieces)

    def finish(low, high):
        own_part, own_log, other_part = attend(
            queries, other_queries, low, high, halves, pieces, state, True
        )
        return own_part, own_log, swap(other_part, "seq", 1)

    done = finish(0, CUT)
    go_right, go_left, att = project_send(
        ((2, 0), (1, 1), (2, 1), (3, 0)), place, *done, out_weight, 2
    )
    got_left = lax.ppermute(go_right, "head", right_x)
    got_right = lax.ppermute(go_left, "head", left_x)

    last_done = finish(CUT, rows)
    go_across, last_att = project_send(
        ((2, 1), (1, 1), (3, 1), (0, 1)), place, *last_done, out_weight, 1
    )
    got_across = swap(go_across, "head", 1)

    kept = project_keep(((1, 0), (3, 1), (0, 0), (0, 1)), place, att, out_weight)
    last_kept = project_keep(((2, 0), (1, 0), (3, 0), (0, 0)), place, last_att, out_weight)

    one = ((CUT, width), BF16)
    to_right, to_left = local(relay_kernel, [one, one], kept, got_left, got_right, name="relay")
    on_right = lax.ppermute(to_right, "head", right_x)
    on_left = lax.ppermute(to_left, "head", left_x)

    m = rows - CUT
    two = ((m, width), BF16)
    last_right, last_left, rest = local(
        spread_kernel, [two, two, ((2 * m, width), F32)], last_kept, got_across, name="spread"
    )
    left2 = lax.ppermute(last_right, "head", right_x)
    right2 = lax.ppermute(last_left, "head", left_x)

    (turned,) = local(turn_kernel, [one], kept, got_left, on_left, name="turn")
    mine_got = swap(turned, "head", 1)

    small = ((m // 2, width), BF16)
    to_right2, to_left2 = local(relay_kernel, [small, small], rest, left2, right2, name="relay")
    on_right2 = lax.ppermute(to_right2, "head", right_x)
    on_left2 = lax.ppermute(to_left2, "head", left_x)
    return local_out(
        last_kernel,
        ((rows, width), BF16),
        kept,
        on_right,
        got_right,
        mine_got,
        rest,
        on_right2,
        on_left2,
        left2,
        right2,
    )


def local_out(kernel, out, *ins):
    return pl.pallas_call(
        kernel,
        in_specs=[IN_VMEM] * len(ins),
        out_specs=IN_VMEM,
        out_shape=jax.ShapeDtypeStruct(*out),
        compiler_params=pltpu.CompilerParams(vmem_limit_bytes=VMEM_LIMIT),
        cost_estimate=LITTLE,
        name="last",
    )(*(held(a) for a in ins))


def solution(mesh):
    placed = (
        P("seq", "head"),
        P("seq", "head"),
        P("seq", "head"),
        P("seq", "head"),
        P("seq", "head"),
        P("head", None),
    )
    return jax.shard_map(
        body, mesh=mesh, in_specs=placed, out_specs=P("seq", "head"), check_vma=False
    )
```

```python
import functools
import math

import jax
import jax.numpy as jnp
from jax import lax
from jax.experimental import pallas as pl
from jax.experimental.pallas import tpu as pltpu
from jax.sharding import PartitionSpec as P

HD = 128
Z = 8
X = 4
BASE2 = math.log2(math.e) / math.sqrt(HD)
F32 = jnp.float32
BF16 = jnp.bfloat16
VMEM_LIMIT = 20 << 20
IN_VMEM = pl.BlockSpec(memory_space=pltpu.VMEM)
CUT = 224
LITTLE = pl.CostEstimate(flops=1, bytes_accessed=1, transcendentals=0)
AFTER_STARTS = pl.CostEstimate(flops=20_000_000_000, bytes_accessed=1, transcendentals=0)


def seq_place(i):
    return i // (2 * Z), (i // 2) % Z, i % 2


def between_frames():
    pairs = []
    for i in range(4 * Z):
        y, z, core = seq_place(i)
        other = (z + 1) % Z if z % 2 else (z - 1) % Z
        pairs.append((i, (y * Z + other) * 2 + core))
    return pairs


def between_frames_across():
    return [(i, to ^ 2 * Z) for i, to in between_frames()]


def along_x(step):
    return [(i, (i // 2 + step) % X * 2 + i % 2) for i in range(2 * X)]


def swap(value, axis, bit):
    return lax.ppermute(value, axis, [(i, i ^ bit) for i in range(lax.axis_size(axis))])


def held(array):
    return pltpu.with_memory_space_constraint(array, pltpu.VMEM)


def local(kernel, outs, *ins, scalars=(), scratch=(), cost=LITTLE, name="local"):
    return pl.pallas_call(
        kernel,
        in_specs=[pl.BlockSpec(memory_space=pltpu.SMEM)] * len(scalars) + [IN_VMEM] * len(ins),
        out_specs=[IN_VMEM] * len(outs),
        out_shape=[pltpu.VMEM(shape, dtype) for shape, dtype in outs],
        scratch_shapes=list(scratch),
        compiler_params=pltpu.CompilerParams(vmem_limit_bytes=VMEM_LIMIT),
        cost_estimate=cost,
        name=name,
    )(*scalars, *(held(a) for a in ins))


def stack_kernel(parts, n_ins, *refs):
    ins, outs, sems = refs[:n_ins], refs[n_ins:-1], refs[-1]
    copies = []
    for out, out_parts in zip(outs, parts):
        at = 0
        for place, low, high in out_parts:
            to = out.at[at : at + high - low, :]
            sem = sems.at[len(copies)]
            copies.append(pltpu.make_async_copy(ins[place].at[low:high, :], to, sem))
            at += high - low
    for copy in copies:
        copy.start()
    for copy in copies:
        copy.wait()


def stacked(arrays, parts=None, cost=LITTLE):
    parts = parts or (tuple((n, 0, a.shape[0]) for n, a in enumerate(arrays)),)
    width, dtype = arrays[0].shape[1], arrays[0].dtype
    return pl.pallas_call(
        functools.partial(stack_kernel, parts, len(arrays)),
        in_specs=[pl.BlockSpec(memory_space=pl.ANY)] * len(arrays),
        out_specs=[IN_VMEM] * len(parts),
        out_shape=[pltpu.VMEM((sum(h - l for _, l, h in part), width), dtype) for part in parts],
        scratch_shapes=[pltpu.SemaphoreType.DMA((sum(len(part) for part in parts),))],
        compiler_params=pltpu.CompilerParams(vmem_limit_bytes=VMEM_LIMIT),
        cost_estimate=cost,
        name="stacked",
    )(*arrays)


def scores_of(rows, keys):
    return lax.dot_general(rows, keys, (((1,), (1,)), ((), ())), preferred_element_type=F32)


def fill_keys(key_ref, value_ref, halves, pieces, columns):
    at = 0
    for half, piece in zip(halves, pieces):
        for low in range(0, piece.shape[0], 2 * half):
            key_ref[at : at + half, :] = piece[low : low + half, columns]
            value_ref[at : at + half, :HD] = piece[low + half : low + 2 * half, columns]
            at += half
    value_ref[:, HD:] = jnp.ones((at, HD), BF16)


def attend_kernel(halves, low, high, with_state, last, *refs):
    queries, refs = refs[:2], refs[2:]
    if with_state:
        (before, before_log), refs = refs[:2], refs[2:]
    pieces, refs = refs[: len(halves)], refs[len(halves) :]
    if last:
        (own_ref, own_log, other_ref, key_ref, value_ref, query_ref, log_ref) = refs
    else:
        (part_ref, log_ref, key_ref, value_ref, query_ref) = refs
    rows = high - low
    heads = queries[0].shape[1] // HD
    for head in range(heads):
        columns = slice(head * HD, (head + 1) * HD)
        slot = head % 2
        fill_keys(key_ref.at[slot], value_ref.at[slot], halves, pieces, columns)
        for place in range(2):
            query_ref[slot, place * rows : (place + 1) * rows, :] = queries[place][low:high, columns]
        scores = scores_of(query_ref[slot], key_ref[slot])
        peak = jnp.max(scores, axis=1, keepdims=True)
        weights = jnp.exp2((scores - peak) * BASE2).astype(BF16)
        both = jnp.dot(weights, value_ref[slot], preferred_element_type=F32)
        summed, total = both[:, :HD], both[:, HD:]
        peak = peak * BASE2
        for place in range(2):
            part = slice(place * rows, (place + 1) * rows)
            if with_state:
                log = before_log[part, head : head + 1]
                top = jnp.maximum(log, peak[part])
                before_factor = jnp.exp2(log - top)
                factor = jnp.exp2(peak[part] - top)
                whole = before_factor + total[part] * factor
                result = (before[part, columns] * before_factor + summed[part] * factor) / whole
            else:
                top = peak[part]
                whole = total[part]
                result = summed[part] / whole
            if last:
                (own_ref, other_ref)[place][:, columns] = result.astype(BF16)
            else:
                part_ref[part, columns] = result
            log_ref[part, head : head + 1] = (top + jnp.log2(whole))[:, :1]
    if last:
        lane = lax.broadcasted_iota(jnp.int32, (rows, HD), 1)
        own_log[...] = log_ref[:rows, :]
        logs = log_ref[rows:, :]
        high_part = logs.astype(BF16).astype(F32)
        rest = logs - high_part
        middle = rest.astype(BF16).astype(F32)
        packed = jnp.where(
            lane < 8,
            high_part,
            jnp.where(lane < 16, pltpu.roll(middle, 8, 1), pltpu.roll(rest - middle, 16, 1)),
        )
        other_ref[:, heads * HD :] = jnp.where(lane < 24, packed, 0.0).astype(BF16)


def attend(queries, other_queries, low, high, halves, pieces, state=None, last=False):
    whole_rows, width = queries.shape
    heads = width // HD
    rows = high - low
    keys = sum(piece.shape[0] for piece in pieces) // 2
    if last:
        outs = [((rows, width), BF16), ((rows, HD), F32), ((rows, width + HD), BF16)]
    else:
        outs = [((2 * rows, width), F32), ((2 * rows, HD), F32)]
    return local(
        functools.partial(attend_kernel, halves, low, high, state is not None, last),
        outs,
        queries,
        other_queries,
        *(state or ()),
        *pieces,
        scratch=[
            pltpu.VMEM((2, keys, HD), BF16),
            pltpu.VMEM((2, keys, 2 * HD), BF16),
            pltpu.VMEM((2, 2 * rows, HD), BF16),
        ]
        + [pltpu.VMEM((2 * rows, HD), F32)] * last,
        cost=LITTLE if last else AFTER_STARTS,
        name="attend_last" if last else "attend_part",
    )


def merge_heads(own, own_log, got, att):
    width = own.shape[1]
    logs = got[:, width:].astype(F32)
    got_log = logs + pltpu.roll(logs, HD - 8, 1) + pltpu.roll(logs, HD - 16, 1)
    for head in range(width // HD):
        columns = slice(head * HD, (head + 1) * HD)
        first, second = own_log[:, head : head + 1], got_log[:, head : head + 1]
        top = jnp.maximum(first, second)
        first_factor = jnp.exp2(first - top)
        second_factor = jnp.exp2(second - top)
        scale = 1.0 / (first_factor + second_factor)
        att[:, columns] = (
            own[:, columns].astype(F32) * (first_factor * scale)
            + got[:, columns].astype(F32) * (second_factor * scale)
        ).astype(BF16)


def products(blocks, place, att, weight, outs):
    rows, width = att.shape
    number = 0
    x, side = place[0] // 2, place[0] % 2
    for out in outs:
        for low in range(0, out.shape[0], rows):
            step, flip = blocks[number]
            block = lax.rem(x + step, X) * 2 + (1 - side if flip else side)
            at = pl.multiple_of(block * width, HD)
            result = jnp.dot(att[...], weight[:, pl.ds(at, width)], preferred_element_type=F32)
            out[low : low + rows, :] = result.astype(out.dtype)
            number += 1


def send_kernel(blocks, place, own, own_log, got, weight, *outs):
    merge_heads(own, own_log, got, outs[-1])
    products(blocks, place, outs[-1], weight, outs[:-1])


def project_send(blocks, place, own, own_log, got, weight, n_outs, cost=LITTLE):
    rows, width = own.shape
    count = len(blocks)
    outs = [((count // n_outs * rows, width), BF16)] * n_outs + [((rows, width), BF16)]
    return local(
        functools.partial(send_kernel, blocks),
        outs,
        own,
        own_log,
        got,
        weight,
        scalars=(place,),
        cost=cost,
        name="project_send",
    )


def keep_kernel(blocks, place, att, weight, out):
    products(blocks, place, att, weight, (out,))


def project_keep(blocks, place, att, weight):
    rows, width = att.shape
    count = len(blocks)
    return local(
        functools.partial(keep_kernel, blocks),
        [((count * rows, width), F32)],
        att,
        weight,
        scalars=(place,),
        name="project_keep",
    )[0]


def relay_kernel(kept, got_left, got_right, to_right, to_left):
    n = got_left.shape[0]
    to_right[:n, :] = (kept[:n, :] + got_left[...].astype(F32)).astype(BF16)
    to_right[n:, :] = kept[n : 2 * n, :].astype(BF16)
    to_left[:n, :] = (kept[2 * n : 3 * n, :] + got_right[...].astype(F32)).astype(BF16)
    to_left[n:, :] = kept[3 * n : 4 * n, :].astype(BF16)


def turn_kernel(kept, on_right, on_left, out):
    n = out.shape[0]
    out[...] = (
        kept[5 * n :, :] + on_left[:n, :].astype(F32) + on_right[n:, :].astype(F32)
    ).astype(BF16)


def spread_kernel(kept, got, *outs):
    m = outs[0].shape[0]
    for number, out in enumerate(outs):
        rows = slice(number * m, (number + 1) * m)
        out[...] = (kept[rows, :] + got[rows, :].astype(F32)).astype(out.dtype)


def total_kernel(first, *refs):
    total = first[...]
    for other in refs[:-1]:
        total = total + other[...].astype(F32)
    refs[-1][...] = total.astype(BF16)


def last_kernel(kept, on_right, on_left, mine, above, out):
    n = mine.shape[0]
    out[:n, :] = (
        kept[4 * n : 5 * n, :]
        + on_right[:n, :].astype(F32)
        + on_left[n:, :].astype(F32)
        + mine[...].astype(F32)
    ).astype(BF16)
    out[n:, :] = above[...]


def body(queries, keys, values, ref_keys, ref_values, out_weight):
    rows, width = queries.shape
    half = ref_keys.shape[0]
    between = between_frames()
    right_x, left_x = along_x(1), along_x(-1)
    place = lax.axis_index("head").reshape(1)
    place, ref_keys = lax.optimization_barrier((place, ref_keys))
    keys, values, ref_keys, ref_values = (
        pltpu.with_memory_space_constraint(a, pltpu.HBM) for a in (keys, values, ref_keys, ref_values)
    )

    (own,) = stacked((ref_keys, ref_values))
    inner = [swap(own, "seq", 2)]
    outer = [lax.ppermute(own, "seq", between)]
    other_queries = swap(queries, "seq", 1)
    (keys, values), own = lax.optimization_barrier(((keys, values), own))
    parts = (rows // 4, rows // 4, rows // 2)
    lows = (0, rows // 4, rows // 2)
    frame = list(stacked(
        (keys, values),
        tuple(
            ((0, low, low + part), (1, low, low + part)) for low, part in zip(lows, parts)
        ),
    ))
    other_frame, across = [swap(frame[0], "seq", 2)], []
    for step in range(3):
        came_inner, came_outer = inner[-1], outer[-1]
        if step:
            came_inner, came_outer, other_frame[step - 1], other_queries = lax.optimization_barrier(
                (came_inner, came_outer, other_frame[step - 1], other_queries)
            )
        if step < 2:
            inner.append(swap(came_outer, "seq", 2))
        outer.append(lax.ppermute(came_inner, "seq", between))
        if step == 2:
            far_across = lax.ppermute(came_inner, "seq", between_frames_across())
        (packed,) = stacked([own] * (step == 0) + [came_inner, came_outer], cost=AFTER_STARTS)
        if step < 2:
            packed, frame[step + 1] = lax.optimization_barrier((packed, frame[step + 1]))
            other_frame.append(swap(frame[step + 1], "seq", 2))
        across.append(swap(packed, "seq", 2 * Z))

    early = (own, *inner[:2], *outer[:2], across[0])

    def attend_early(low, high):
        return attend(
            queries,
            other_queries,
            low,
            high,
            parts + parts[:2] + (half,) * len(early),
            (*frame, *other_frame[:2], *early),
        )

    state = attend_early(0, CUT)
    last_state = attend_early(CUT, rows)
    state, last_state = lax.optimization_barrier((state, last_state))
    pieces = (inner[2], *outer[2:], far_across, *across[1:], *other_frame[2:])
    halves = (half,) * (len(pieces) - 1) + parts[2:]

    def finish(low, high, state):
        own_part, own_log, other_part = attend(
            queries, other_queries, low, high, halves, pieces, state, True
        )
        return own_part, own_log, swap(other_part, "seq", 1)

    done = finish(0, CUT, state)
    go_right, go_left, att = project_send(((2, 0), (2, 1)), place, *done, out_weight, 2)

    last_done = finish(CUT, rows, last_state)
    last_done, go_right, go_left = lax.optimization_barrier((last_done, go_right, go_left))
    got_left = lax.ppermute(go_right, "head", right_x)
    got_right = lax.ppermute(go_left, "head", left_x)
    go_across, last_att = project_send(
        ((2, 1), (1, 1), (3, 1), (0, 1)), place, *last_done, out_weight, 1, AFTER_STARTS
    )
    got_across = swap(go_across, "head", 1)

    att, last_att = lax.optimization_barrier((att, last_att))
    kept = project_keep(
        ((1, 0), (1, 1), (3, 1), (3, 0), (0, 0), (0, 1)), place, att, out_weight
    )
    last_kept = project_keep(
        ((2, 0), (1, 0), (3, 0), (0, 0)), place, last_att, out_weight
    )

    two = ((2 * CUT, width), BF16)
    to_right, to_left = local(relay_kernel, [two, two], kept, got_left, got_right, name="relay")
    on_right = lax.ppermute(to_right, "head", right_x)
    on_left = lax.ppermute(to_left, "head", left_x)

    part = (rows - CUT, width)
    *spread, rest = local(
        spread_kernel, [(part, BF16)] * 3 + [(part, F32)], last_kept, got_across, name="spread"
    )
    on_left, on_right, spread, rest = lax.optimization_barrier((on_left, on_right, spread, rest))
    others = [lax.ppermute(a, "head", along_x(step)) for a, step in zip(spread, (2, 1, X - 1))]
    (turned,) = local(
        turn_kernel, [((CUT, width), BF16)], kept, on_right, on_left, cost=AFTER_STARTS, name="turn"
    )
    mine_got = swap(turned, "head", 1)
    (above,) = local(total_kernel, [(part, BF16)], rest, *others, cost=AFTER_STARTS, name="total")
    return local_out(
        last_kernel, ((rows, width), BF16), kept, on_right, on_left, mine_got, above
    )


def local_out(kernel, out, *ins):
    return pl.pallas_call(
        kernel,
        in_specs=[IN_VMEM] * len(ins),
        out_specs=IN_VMEM,
        out_shape=jax.ShapeDtypeStruct(*out),
        compiler_params=pltpu.CompilerParams(vmem_limit_bytes=VMEM_LIMIT),
        cost_estimate=LITTLE,
        name="last",
    )(*(held(a) for a in ins))


def solution(mesh):
    placed = (
        P("seq", "head"),
        P("seq", "head"),
        P("seq", "head"),
        P("seq", "head"),
        P("seq", "head"),
        P("head", None),
    )
    return jax.shard_map(
        body, mesh=mesh, in_specs=placed, out_specs=P("seq", "head"), check_vma=False
    )
```

```python
import functools
import math

import jax
import jax.numpy as jnp
from jax import lax
from jax.experimental import pallas as pl
from jax.experimental.pallas import tpu as pltpu
from jax.sharding import PartitionSpec as P

HD = 128
Z = 8
X = 4
BASE2 = math.log2(math.e) / math.sqrt(HD)
F32 = jnp.float32
BF16 = jnp.bfloat16
VMEM_LIMIT = 20 << 20
IN_VMEM = pl.BlockSpec(memory_space=pltpu.VMEM)
CUT = 256
AHEAD_ROWS = 160
LITTLE = pl.CostEstimate(flops=1, bytes_accessed=1, transcendentals=0)
AFTER_STARTS = pl.CostEstimate(flops=20_000_000_000, bytes_accessed=1, transcendentals=0)


def seq_place(i):
    return i // (2 * Z), (i // 2) % Z, i % 2


def between_frames():
    pairs = []
    for i in range(4 * Z):
        y, z, core = seq_place(i)
        other = (z + 1) % Z if z % 2 else (z - 1) % Z
        pairs.append((i, (y * Z + other) * 2 + core))
    return pairs


def between_frames_across():
    return [(i, to ^ 2 * Z) for i, to in between_frames()]


def along_x(step):
    return [(i, (i // 2 + step) % X * 2 + i % 2) for i in range(2 * X)]


def swap(value, axis, bit):
    return lax.ppermute(value, axis, [(i, i ^ bit) for i in range(lax.axis_size(axis))])


def held(array):
    return pltpu.with_memory_space_constraint(array, pltpu.VMEM)


def local(kernel, outs, *ins, scalars=(), scratch=(), cost=LITTLE, name="local"):
    return pl.pallas_call(
        kernel,
        in_specs=[pl.BlockSpec(memory_space=pltpu.SMEM)] * len(scalars) + [IN_VMEM] * len(ins),
        out_specs=[IN_VMEM] * len(outs),
        out_shape=[pltpu.VMEM(shape, dtype) for shape, dtype in outs],
        scratch_shapes=list(scratch),
        compiler_params=pltpu.CompilerParams(vmem_limit_bytes=VMEM_LIMIT),
        cost_estimate=cost,
        name=name,
    )(*scalars, *(held(a) for a in ins))


def stack_kernel(parts, n_ins, *refs):
    ins, outs, sems = refs[:n_ins], refs[n_ins:-1], refs[-1]
    copies = []
    for out, out_parts in zip(outs, parts):
        at = 0
        for place, low, high in out_parts:
            to = out.at[at : at + high - low, :]
            sem = sems.at[len(copies)]
            copies.append(pltpu.make_async_copy(ins[place].at[low:high, :], to, sem))
            at += high - low
    for copy in copies:
        copy.start()
    for copy in copies:
        copy.wait()


def stacked(arrays, parts=None, cost=LITTLE):
    parts = parts or (tuple((n, 0, a.shape[0]) for n, a in enumerate(arrays)),)
    width, dtype = arrays[0].shape[1], arrays[0].dtype
    return pl.pallas_call(
        functools.partial(stack_kernel, parts, len(arrays)),
        in_specs=[pl.BlockSpec(memory_space=pl.ANY)] * len(arrays),
        out_specs=[IN_VMEM] * len(parts),
        out_shape=[pltpu.VMEM((sum(h - l for _, l, h in part), width), dtype) for part in parts],
        scratch_shapes=[pltpu.SemaphoreType.DMA((sum(len(part) for part in parts),))],
        compiler_params=pltpu.CompilerParams(vmem_limit_bytes=VMEM_LIMIT),
        cost_estimate=cost,
        name="stacked",
    )(*arrays)


def scores_of(rows, keys):
    return lax.dot_general(rows, keys, (((1,), (1,)), ((), ())), preferred_element_type=F32)


def fill_keys(key_ref, value_ref, halves, pieces, columns):
    at = 0
    for half, piece in zip(halves, pieces):
        for low in range(0, piece.shape[0], 2 * half):
            key_ref[at : at + half, :] = piece[low : low + half, columns]
            value_ref[at : at + half, :HD] = piece[low + half : low + 2 * half, columns]
            at += half
    value_ref[:, HD:] = jnp.ones((at, HD), BF16)


def attend_kernel(halves, low, high, with_state, last, *refs):
    queries, refs = refs[:2], refs[2:]
    if with_state:
        (before, before_log), refs = refs[:2], refs[2:]
    pieces, refs = refs[: len(halves)], refs[len(halves) :]
    if last:
        (own_ref, own_log, other_ref, key_ref, value_ref, query_ref, log_ref) = refs
    else:
        (part_ref, log_ref, key_ref, value_ref, query_ref) = refs
    rows = high - low
    heads = queries[0].shape[1] // HD

    def scores_for(head):
        columns = slice(head * HD, (head + 1) * HD)
        slot = head % 2
        fill_keys(key_ref.at[slot], value_ref.at[slot], halves, pieces, columns)
        for place in range(2):
            query_ref[slot, place * rows : (place + 1) * rows, :] = queries[place][low:high, columns]
        return scores_of(query_ref[slot], key_ref[slot])

    ahead = rows <= AHEAD_ROWS
    next_scores = scores_for(0)
    for head in range(heads):
        columns = slice(head * HD, (head + 1) * HD)
        slot = head % 2
        scores = next_scores
        if ahead and head + 1 < heads:
            next_scores = scores_for(head + 1)
        peak = jnp.max(scores, axis=1, keepdims=True)
        weights = jnp.exp2((scores - peak) * BASE2).astype(BF16)
        both = jnp.dot(weights, value_ref[slot], preferred_element_type=F32)
        if not ahead and head + 1 < heads:
            next_scores = scores_for(head + 1)
        summed, total = both[:, :HD], both[:, HD:]
        peak = peak * BASE2
        for place in range(2):
            part = slice(place * rows, (place + 1) * rows)
            if with_state:
                log = before_log[part, head : head + 1]
                top = jnp.maximum(log, peak[part])
                before_factor = jnp.exp2(log - top)
                factor = jnp.exp2(peak[part] - top)
                whole = before_factor + total[part] * factor
                result = (before[part, columns] * before_factor + summed[part] * factor) / whole
            else:
                top = peak[part]
                whole = total[part]
                result = summed[part] / whole
            if last:
                (own_ref, other_ref)[place][:, columns] = result.astype(BF16)
            else:
                part_ref[part, columns] = result
            log_ref[part, head : head + 1] = (top + jnp.log2(whole))[:, :1]
    if last:
        lane = lax.broadcasted_iota(jnp.int32, (rows, HD), 1)
        own_log[...] = log_ref[:rows, :]
        logs = log_ref[rows:, :]
        high_part = logs.astype(BF16).astype(F32)
        rest = logs - high_part
        middle = rest.astype(BF16).astype(F32)
        packed = jnp.where(
            lane < 8,
            high_part,
            jnp.where(lane < 16, pltpu.roll(middle, 8, 1), pltpu.roll(rest - middle, 16, 1)),
        )
        other_ref[:, heads * HD :] = jnp.where(lane < 24, packed, 0.0).astype(BF16)


def attend(queries, other_queries, low, high, halves, pieces, state=None, last=False):
    whole_rows, width = queries.shape
    heads = width // HD
    rows = high - low
    keys = sum(piece.shape[0] for piece in pieces) // 2
    if last:
        outs = [((rows, width), BF16), ((rows, HD), F32), ((rows, width + HD), BF16)]
    else:
        outs = [((2 * rows, width), F32), ((2 * rows, HD), F32)]
    return local(
        functools.partial(attend_kernel, halves, low, high, state is not None, last),
        outs,
        queries,
        other_queries,
        *(state or ()),
        *pieces,
        scratch=[
            pltpu.VMEM((2, keys, HD), BF16),
            pltpu.VMEM((2, keys, 2 * HD), BF16),
            pltpu.VMEM((2, 2 * rows, HD), BF16),
        ]
        + [pltpu.VMEM((2 * rows, HD), F32)] * last,
        cost=LITTLE if last else AFTER_STARTS,
        name="attend_last" if last else "attend_part",
    )


def merge_heads(own, own_log, got, att):
    width = own.shape[1]
    logs = got[:, width:].astype(F32)
    got_log = logs + pltpu.roll(logs, HD - 8, 1) + pltpu.roll(logs, HD - 16, 1)
    for head in range(width // HD):
        columns = slice(head * HD, (head + 1) * HD)
        first, second = own_log[:, head : head + 1], got_log[:, head : head + 1]
        top = jnp.maximum(first, second)
        first_factor = jnp.exp2(first - top)
        second_factor = jnp.exp2(second - top)
        scale = 1.0 / (first_factor + second_factor)
        att[:, columns] = (
            own[:, columns].astype(F32) * (first_factor * scale)
            + got[:, columns].astype(F32) * (second_factor * scale)
        ).astype(BF16)


def products(blocks, place, att, weight, outs):
    rows, width = att.shape
    number = 0
    x, side = place[0] // 2, place[0] % 2
    for out in outs:
        for low in range(0, out.shape[0], rows):
            step, flip = blocks[number]
            block = lax.rem(x + step, X) * 2 + (1 - side if flip else side)
            at = pl.multiple_of(block * width, HD)
            result = jnp.dot(att[...], weight[:, pl.ds(at, width)], preferred_element_type=F32)
            out[low : low + rows, :] = result.astype(out.dtype)
            number += 1


def send_kernel(blocks, place, own, own_log, got, weight, *outs):
    merge_heads(own, own_log, got, outs[-1])
    products(blocks, place, outs[-1], weight, outs[:-1])


def project_send(blocks, place, own, own_log, got, weight, n_outs, cost=LITTLE):
    rows, width = own.shape
    count = len(blocks)
    outs = [((count // n_outs * rows, width), BF16)] * n_outs + [((rows, width), BF16)]
    return local(
        functools.partial(send_kernel, blocks),
        outs,
        own,
        own_log,
        got,
        weight,
        scalars=(place,),
        cost=cost,
        name="project_send",
    )


def keep_kernel(blocks, place, att, weight, *outs):
    products(blocks, place, att, weight, outs)


def project_keep(blocks, place, att, weight, n_outs=1, dtype=F32):
    rows, width = att.shape
    return local(
        functools.partial(keep_kernel, blocks),
        [((len(blocks) // n_outs * rows, width), dtype)] * n_outs,
        att,
        weight,
        scalars=(place,),
        name="project_keep",
    )


def relay_kernel(kept, got_left, got_right, to_right, to_left):
    n = got_left.shape[0]
    to_right[...] = (kept[:n, :] + got_left[...].astype(F32)).astype(BF16)
    to_left[...] = (kept[n : 2 * n, :] + got_right[...].astype(F32)).astype(BF16)


def turn_kernel(kept, next_left, on_left, out):
    n = out.shape[0]
    out[...] = (
        kept[3 * n :, :] + on_left[...].astype(F32) + next_left[...].astype(F32)
    ).astype(BF16)


def spread_kernel(kept, got, *outs):
    m = outs[0].shape[0]
    for number, out in enumerate(outs):
        rows = slice(number * m, (number + 1) * m)
        out[...] = (kept[rows, :] + got[rows, :].astype(F32)).astype(out.dtype)


def below_kernel(kept, on_right, next_right, mine, out):
    n = mine.shape[0]
    out[...] = (
        kept[2 * n : 3 * n, :]
        + on_right[...].astype(F32)
        + next_right[...].astype(F32)
        + mine[...].astype(F32)
    ).astype(BF16)


def last_kernel(below, rest, *refs):
    others, out = refs[:-1], refs[-1]
    n = below.shape[0]
    out[:n, :] = below[...]
    total = rest[...]
    for other in others:
        total = total + other[...].astype(F32)
    out[n:, :] = total.astype(BF16)


def body(queries, keys, values, ref_keys, ref_values, out_weight):
    rows, width = queries.shape
    half = ref_keys.shape[0]
    between = between_frames()
    right_x, left_x = along_x(1), along_x(-1)
    place = lax.axis_index("head").reshape(1)
    place, ref_keys = lax.optimization_barrier((place, ref_keys))
    keys, values, ref_keys, ref_values = (
        pltpu.with_memory_space_constraint(a, pltpu.HBM) for a in (keys, values, ref_keys, ref_values)
    )

    (own,) = stacked((ref_keys, ref_values))
    inner = [swap(own, "seq", 2)]
    outer = [lax.ppermute(own, "seq", between)]
    other_queries = swap(queries, "seq", 1)
    (keys, values), own = lax.optimization_barrier(((keys, values), own))
    parts = (rows // 4, rows // 4, rows // 2)
    lows = (0, rows // 4, rows // 2)
    frame = list(stacked(
        (keys, values),
        tuple(
            ((0, low, low + part), (1, low, low + part)) for low, part in zip(lows, parts)
        ),
    ))
    other_frame, across = [swap(frame[0], "seq", 2)], []
    for step in range(3):
        came_inner, came_outer = inner[-1], outer[-1]
        if step:
            came_inner, came_outer, other_frame[step - 1], other_queries = lax.optimization_barrier(
                (came_inner, came_outer, other_frame[step - 1], other_queries)
            )
        if step < 2:
            inner.append(swap(came_outer, "seq", 2))
        outer.append(lax.ppermute(came_inner, "seq", between))
        if step == 2:
            far_across = lax.ppermute(came_inner, "seq", between_frames_across())
        (packed,) = stacked([own] * (step == 0) + [came_inner, came_outer], cost=AFTER_STARTS)
        if step < 2:
            packed, frame[step + 1] = lax.optimization_barrier((packed, frame[step + 1]))
            other_frame.append(swap(frame[step + 1], "seq", 2))
        across.append(swap(packed, "seq", 2 * Z))

    early = (own, *inner[:2], *outer[:2], across[0])

    def attend_early(low, high):
        return attend(
            queries,
            other_queries,
            low,
            high,
            parts + parts[:2] + (half,) * len(early),
            (*frame, *other_frame[:2], *early),
        )

    state = attend_early(0, CUT)
    last_state = attend_early(CUT, rows)
    state, last_state = lax.optimization_barrier((state, last_state))
    pieces = (inner[2], *outer[2:], far_across, *across[1:], *other_frame[2:])
    halves = (half,) * (len(pieces) - 1) + parts[2:]

    def finish(low, high, state):
        own_part, own_log, other_part = attend(
            queries, other_queries, low, high, halves, pieces, state, True
        )
        return own_part, own_log, swap(other_part, "seq", 1)

    done = finish(0, CUT, state)
    go_right, go_left, att = project_send(((2, 0), (2, 1)), place, *done, out_weight, 2)

    last_done = finish(CUT, rows, last_state)
    last_done, go_right, go_left = lax.optimization_barrier((last_done, go_right, go_left))
    go_across, last_att = project_send(
        ((2, 1), (1, 1), (3, 1), (0, 1)), place, *last_done, out_weight, 1, AFTER_STARTS
    )
    got_across = swap(go_across, "head", 1)
    got_right = lax.ppermute(go_left, "head", left_x)
    got_left = lax.ppermute(go_right, "head", right_x)

    att, last_att = lax.optimization_barrier((att, last_att))
    next_go_right, next_go_left = project_keep(((1, 1), (3, 0)), place, att, out_weight, 2, BF16)
    next_left = lax.ppermute(next_go_right, "head", right_x)
    next_right = lax.ppermute(next_go_left, "head", left_x)
    att, next_go_right = lax.optimization_barrier((att, next_go_right))
    (kept,) = project_keep(((1, 0), (3, 1), (0, 0), (0, 1)), place, att, out_weight)

    one = ((CUT, width), BF16)
    to_right, to_left = local(relay_kernel, [one, one], kept, got_left, got_right, name="relay")
    on_right = lax.ppermute(to_right, "head", right_x)
    on_left = lax.ppermute(to_left, "head", left_x)

    last_att, next_left, next_right = lax.optimization_barrier((last_att, next_left, next_right))
    (last_kept,) = project_keep(
        ((2, 0), (1, 0), (3, 0), (0, 0)), place, last_att, out_weight
    )
    part = (rows - CUT, width)
    *spread, rest = local(
        spread_kernel, [(part, BF16)] * 3 + [(part, F32)], last_kept, got_across, name="spread"
    )
    others = [lax.ppermute(a, "head", along_x(step)) for a, step in zip(spread, (2, 1, X - 1))]
    kept, rest, on_left, on_right = lax.optimization_barrier((kept, rest, on_left, on_right))
    (turned,) = local(
        turn_kernel, [((CUT, width), BF16)], kept, next_left, on_left, cost=AFTER_STARTS, name="turn"
    )
    mine_got = swap(turned, "head", 1)
    (below,) = local(
        below_kernel,
        [((CUT, width), BF16)],
        kept,
        on_right,
        next_right,
        mine_got,
        cost=AFTER_STARTS,
        name="below",
    )
    return local_out(last_kernel, ((rows, width), BF16), below, rest, *others)


def local_out(kernel, out, *ins):
    return pl.pallas_call(
        kernel,
        in_specs=[IN_VMEM] * len(ins),
        out_specs=IN_VMEM,
        out_shape=jax.ShapeDtypeStruct(*out),
        compiler_params=pltpu.CompilerParams(vmem_limit_bytes=VMEM_LIMIT),
        cost_estimate=LITTLE,
        name="last",
    )(*(held(a) for a in ins))


def solution(mesh):
    placed = (
        P("seq", "head"),
        P("seq", "head"),
        P("seq", "head"),
        P("seq", "head"),
        P("seq", "head"),
        P("head", None),
    )
    return jax.shard_map(
        body, mesh=mesh, in_specs=placed, out_specs=P("seq", "head"), check_vma=False
    )
```

```python
import functools
import math

import jax
import jax.numpy as jnp
from jax import lax
from jax.experimental import pallas as pl
from jax.experimental.pallas import tpu as pltpu
from jax.sharding import PartitionSpec as P

HD = 128
Z = 8
X = 4
BASE2 = math.log2(math.e) / math.sqrt(HD)
F32 = jnp.float32
BF16 = jnp.bfloat16
VMEM_LIMIT = 20 << 20
IN_VMEM = pl.BlockSpec(memory_space=pltpu.VMEM)
CUT = 256
LITTLE = pl.CostEstimate(flops=1, bytes_accessed=1, transcendentals=0)
AFTER_STARTS = pl.CostEstimate(flops=20_000_000_000, bytes_accessed=1, transcendentals=0)


def seq_place(i):
    return i // (2 * Z), (i // 2) % Z, i % 2


def between_frames():
    pairs = []
    for i in range(4 * Z):
        y, z, core = seq_place(i)
        other = (z + 1) % Z if z % 2 else (z - 1) % Z
        pairs.append((i, (y * Z + other) * 2 + core))
    return pairs


def between_frames_across():
    return [(i, to ^ 2 * Z) for i, to in between_frames()]


def along_x(step):
    return [(i, (i // 2 + step) % X * 2 + i % 2) for i in range(2 * X)]


def swap(value, axis, bit):
    return lax.ppermute(value, axis, [(i, i ^ bit) for i in range(lax.axis_size(axis))])


def held(array):
    return pltpu.with_memory_space_constraint(array, pltpu.VMEM)


def local(kernel, outs, *ins, scalars=(), scratch=(), cost=LITTLE, name="local"):
    return pl.pallas_call(
        kernel,
        in_specs=[pl.BlockSpec(memory_space=pltpu.SMEM)] * len(scalars) + [IN_VMEM] * len(ins),
        out_specs=[IN_VMEM] * len(outs),
        out_shape=[pltpu.VMEM(shape, dtype) for shape, dtype in outs],
        scratch_shapes=list(scratch),
        compiler_params=pltpu.CompilerParams(vmem_limit_bytes=VMEM_LIMIT),
        cost_estimate=cost,
        name=name,
    )(*scalars, *(held(a) for a in ins))


def stack_kernel(parts, n_ins, *refs):
    ins, outs, sems = refs[:n_ins], refs[n_ins:-1], refs[-1]
    copies = []
    for out, out_parts in zip(outs, parts):
        at = 0
        for place, low, high in out_parts:
            to = out.at[at : at + high - low, :]
            sem = sems.at[len(copies)]
            copies.append(pltpu.make_async_copy(ins[place].at[low:high, :], to, sem))
            at += high - low
    for copy in copies:
        copy.start()
    for copy in copies:
        copy.wait()


def stacked(arrays, parts=None, cost=LITTLE):
    parts = parts or (tuple((n, 0, a.shape[0]) for n, a in enumerate(arrays)),)
    width, dtype = arrays[0].shape[1], arrays[0].dtype
    return pl.pallas_call(
        functools.partial(stack_kernel, parts, len(arrays)),
        in_specs=[pl.BlockSpec(memory_space=pl.ANY)] * len(arrays),
        out_specs=[IN_VMEM] * len(parts),
        out_shape=[pltpu.VMEM((sum(h - l for _, l, h in part), width), dtype) for part in parts],
        scratch_shapes=[pltpu.SemaphoreType.DMA((sum(len(part) for part in parts),))],
        compiler_params=pltpu.CompilerParams(vmem_limit_bytes=VMEM_LIMIT),
        cost_estimate=cost,
        name="stacked",
    )(*arrays)


def scores_of(rows, keys):
    return lax.dot_general(rows, keys, (((1,), (1,)), ((), ())), preferred_element_type=F32)


def fill_keys(key_ref, value_ref, halves, pieces, columns):
    at = 0
    for half, piece in zip(halves, pieces):
        for low in range(0, piece.shape[0], 2 * half):
            key_ref[at : at + half, :] = piece[low : low + half, columns]
            value_ref[at : at + half, :HD] = piece[low + half : low + 2 * half, columns]
            at += half
    value_ref[:, HD:] = jnp.ones((at, HD), BF16)


def attend_kernel(halves, low, high, with_state, last, *refs):
    queries, refs = refs[:2], refs[2:]
    if with_state:
        (before, before_log), refs = refs[:2], refs[2:]
    pieces, refs = refs[: len(halves)], refs[len(halves) :]
    if last:
        (own_ref, own_log, other_ref, key_ref, value_ref, query_ref, log_ref) = refs
    else:
        (part_ref, log_ref, key_ref, value_ref, query_ref) = refs
    rows = high - low
    heads = queries[0].shape[1] // HD

    def scores_for(head):
        columns = slice(head * HD, (head + 1) * HD)
        slot = head % 2
        fill_keys(key_ref.at[slot], value_ref.at[slot], halves, pieces, columns)
        for place in range(2):
            query_ref[slot, place * rows : (place + 1) * rows, :] = queries[place][low:high, columns]
        return scores_of(query_ref[slot], key_ref[slot])

    next_scores = scores_for(0)
    for head in range(heads):
        columns = slice(head * HD, (head + 1) * HD)
        slot = head % 2
        scores = next_scores
        if head + 1 < heads:
            next_scores = scores_for(head + 1)
        peak = jnp.max(scores, axis=1, keepdims=True)
        weights = jnp.exp2((scores - peak) * BASE2).astype(BF16)
        both = jnp.dot(weights, value_ref[slot], preferred_element_type=F32)
        summed, total = both[:, :HD], both[:, HD:]
        peak = peak * BASE2
        for place in range(2):
            part = slice(place * rows, (place + 1) * rows)
            if with_state:
                log = before_log[part, head : head + 1]
                top = jnp.maximum(log, peak[part])
                before_factor = jnp.exp2(log - top)
                factor = jnp.exp2(peak[part] - top)
                whole = before_factor + total[part] * factor
                result = (before[part, columns] * before_factor + summed[part] * factor) / whole
            else:
                top = peak[part]
                whole = total[part]
                result = summed[part] / whole
            if last:
                (own_ref, other_ref)[place][:, columns] = result.astype(BF16)
            else:
                part_ref[part, columns] = result
            log_ref[part, head : head + 1] = (top + jnp.log2(whole))[:, :1]
    if last:
        lane = lax.broadcasted_iota(jnp.int32, (rows, HD), 1)
        own_log[...] = log_ref[:rows, :]
        logs = log_ref[rows:, :]
        high_part = logs.astype(BF16).astype(F32)
        rest = logs - high_part
        middle = rest.astype(BF16).astype(F32)
        packed = jnp.where(
            lane < 8,
            high_part,
            jnp.where(lane < 16, pltpu.roll(middle, 8, 1), pltpu.roll(rest - middle, 16, 1)),
        )
        other_ref[:, heads * HD :] = jnp.where(lane < 24, packed, 0.0).astype(BF16)


def attend(queries, other_queries, low, high, halves, pieces, state=None, last=False):
    whole_rows, width = queries.shape
    heads = width // HD
    rows = high - low
    keys = sum(piece.shape[0] for piece in pieces) // 2
    if last:
        outs = [((rows, width), BF16), ((rows, HD), F32), ((rows, width + HD), BF16)]
    else:
        outs = [((2 * rows, width), F32), ((2 * rows, HD), F32)]
    return local(
        functools.partial(attend_kernel, halves, low, high, state is not None, last),
        outs,
        queries,
        other_queries,
        *(state or ()),
        *pieces,
        scratch=[
            pltpu.VMEM((2, keys, HD), BF16),
            pltpu.VMEM((2, keys, 2 * HD), BF16),
            pltpu.VMEM((2, 2 * rows, HD), BF16),
        ]
        + [pltpu.VMEM((2 * rows, HD), F32)] * last,
        cost=LITTLE if last else AFTER_STARTS,
        name="attend_last" if last else "attend_part",
    )


def merge_heads(own, own_log, got, att):
    width = own.shape[1]
    logs = got[:, width:].astype(F32)
    got_log = logs + pltpu.roll(logs, HD - 8, 1) + pltpu.roll(logs, HD - 16, 1)
    for head in range(width // HD):
        columns = slice(head * HD, (head + 1) * HD)
        first, second = own_log[:, head : head + 1], got_log[:, head : head + 1]
        top = jnp.maximum(first, second)
        first_factor = jnp.exp2(first - top)
        second_factor = jnp.exp2(second - top)
        scale = 1.0 / (first_factor + second_factor)
        att[:, columns] = (
            own[:, columns].astype(F32) * (first_factor * scale)
            + got[:, columns].astype(F32) * (second_factor * scale)
        ).astype(BF16)


def products(blocks, place, att, weight, outs):
    rows, width = att.shape
    number = 0
    x, side = place[0] // 2, place[0] % 2
    for out in outs:
        for low in range(0, out.shape[0], rows):
            step, flip = blocks[number]
            block = lax.rem(x + step, X) * 2 + (1 - side if flip else side)
            at = pl.multiple_of(block * width, HD)
            result = jnp.dot(att[...], weight[:, pl.ds(at, width)], preferred_element_type=F32)
            out[low : low + rows, :] = result.astype(out.dtype)
            number += 1


def send_kernel(blocks, place, own, own_log, got, weight, *outs):
    merge_heads(own, own_log, got, outs[-1])
    products(blocks, place, outs[-1], weight, outs[:-1])


def project_send(blocks, place, own, own_log, got, weight, n_outs, cost=LITTLE):
    rows, width = own.shape
    count = len(blocks)
    outs = [((count // n_outs * rows, width), BF16)] * n_outs + [((rows, width), BF16)]
    return local(
        functools.partial(send_kernel, blocks),
        outs,
        own,
        own_log,
        got,
        weight,
        scalars=(place,),
        cost=cost,
        name="project_send",
    )


def keep_kernel(blocks, place, att, weight, *outs):
    products(blocks, place, att, weight, outs)


def project_keep(blocks, place, att, weight, n_outs=1, dtype=F32):
    rows, width = att.shape
    return local(
        functools.partial(keep_kernel, blocks),
        [((len(blocks) // n_outs * rows, width), dtype)] * n_outs,
        att,
        weight,
        scalars=(place,),
        name="project_keep",
    )


def relay_kernel(kept, got_left, got_right, to_right, to_left):
    n = got_left.shape[0]
    to_right[...] = (kept[:n, :] + got_left[...].astype(F32)).astype(BF16)
    to_left[...] = (kept[n : 2 * n, :] + got_right[...].astype(F32)).astype(BF16)


def turn_kernel(kept, next_left, on_left, out):
    n = out.shape[0]
    out[...] = (
        kept[3 * n :, :] + on_left[...].astype(F32) + next_left[...].astype(F32)
    ).astype(BF16)


def spread_kernel(kept, got, *outs):
    m = outs[0].shape[0]
    for number, out in enumerate(outs):
        rows = slice(number * m, (number + 1) * m)
        out[...] = (kept[rows, :] + got[rows, :].astype(F32)).astype(out.dtype)


def below_kernel(kept, on_right, next_right, mine, out):
    n = mine.shape[0]
    out[...] = (
        kept[2 * n : 3 * n, :]
        + on_right[...].astype(F32)
        + next_right[...].astype(F32)
        + mine[...].astype(F32)
    ).astype(BF16)


def last_kernel(below, rest, *refs):
    others, out = refs[:-1], refs[-1]
    n = below.shape[0]
    out[:n, :] = below[...]
    total = rest[...]
    for other in others:
        total = total + other[...].astype(F32)
    out[n:, :] = total.astype(BF16)


def body(queries, keys, values, ref_keys, ref_values, out_weight):
    rows, width = queries.shape
    half = ref_keys.shape[0]
    between = between_frames()
    right_x, left_x = along_x(1), along_x(-1)
    place = lax.axis_index("head").reshape(1)
    place, ref_keys = lax.optimization_barrier((place, ref_keys))
    keys, values, ref_keys, ref_values = (
        pltpu.with_memory_space_constraint(a, pltpu.HBM) for a in (keys, values, ref_keys, ref_values)
    )

    (own,) = stacked((ref_keys, ref_values))
    inner = [swap(own, "seq", 2)]
    outer = [lax.ppermute(own, "seq", between)]
    other_queries = swap(queries, "seq", 1)
    (keys, values), own = lax.optimization_barrier(((keys, values), own))
    parts = (rows // 4, rows // 4, rows // 2)
    lows = (0, rows // 4, rows // 2)
    frame = list(stacked(
        (keys, values),
        tuple(
            ((0, low, low + part), (1, low, low + part)) for low, part in zip(lows, parts)
        ),
    ))
    other_frame, across = [swap(frame[0], "seq", 2)], []
    for step in range(3):
        came_inner, came_outer = inner[-1], outer[-1]
        if step:
            came_inner, came_outer, other_frame[step - 1], other_queries = lax.optimization_barrier(
                (came_inner, came_outer, other_frame[step - 1], other_queries)
            )
        if step < 2:
            inner.append(swap(came_outer, "seq", 2))
        outer.append(lax.ppermute(came_inner, "seq", between))
        if step == 2:
            far_across = lax.ppermute(came_inner, "seq", between_frames_across())
        (packed,) = stacked([own] * (step == 0) + [came_inner, came_outer], cost=AFTER_STARTS)
        if step < 2:
            packed, frame[step + 1] = lax.optimization_barrier((packed, frame[step + 1]))
            other_frame.append(swap(frame[step + 1], "seq", 2))
        across.append(swap(packed, "seq", 2 * Z))

    early = (own, *inner[:2], *outer[:2], across[0])

    def attend_early(low, high):
        return attend(
            queries,
            other_queries,
            low,
            high,
            parts + parts[:2] + (half,) * len(early),
            (*frame, *other_frame[:2], *early),
        )

    state = attend_early(0, CUT)
    last_state = attend_early(CUT, rows)
    state, last_state = lax.optimization_barrier((state, last_state))
    pieces = (inner[2], *outer[2:], far_across, *across[1:], *other_frame[2:])
    halves = (half,) * (len(pieces) - 1) + parts[2:]

    def finish(low, high, state):
        own_part, own_log, other_part = attend(
            queries, other_queries, low, high, halves, pieces, state, True
        )
        return own_part, own_log, swap(other_part, "seq", 1)

    done = finish(0, CUT, state)
    go_right, go_left, att = project_send(((2, 0), (2, 1)), place, *done, out_weight, 2)

    last_done = finish(CUT, rows, last_state)
    last_done, go_right, go_left = lax.optimization_barrier((last_done, go_right, go_left))
    go_across, last_att = project_send(
        ((2, 1), (1, 1), (3, 1), (0, 1)), place, *last_done, out_weight, 1, AFTER_STARTS
    )
    got_across = swap(go_across, "head", 1)
    got_right = lax.ppermute(go_left, "head", left_x)
    got_left = lax.ppermute(go_right, "head", right_x)

    att, last_att = lax.optimization_barrier((att, last_att))
    next_go_right, next_go_left = project_keep(((1, 1), (3, 0)), place, att, out_weight, 2, BF16)
    next_left = lax.ppermute(next_go_right, "head", right_x)
    next_right = lax.ppermute(next_go_left, "head", left_x)
    att, next_go_right = lax.optimization_barrier((att, next_go_right))
    (kept,) = project_keep(((1, 0), (3, 1), (0, 0), (0, 1)), place, att, out_weight)

    one = ((CUT, width), BF16)
    to_right, to_left = local(relay_kernel, [one, one], kept, got_left, got_right, name="relay")
    on_right = lax.ppermute(to_right, "head", right_x)
    on_left = lax.ppermute(to_left, "head", left_x)

    last_att, next_left, next_right = lax.optimization_barrier((last_att, next_left, next_right))
    (last_kept,) = project_keep(
        ((2, 0), (1, 0), (3, 0), (0, 0)), place, last_att, out_weight
    )
    part = (rows - CUT, width)
    *spread, rest = local(
        spread_kernel, [(part, BF16)] * 3 + [(part, F32)], last_kept, got_across, name="spread"
    )
    others = [lax.ppermute(a, "head", along_x(step)) for a, step in zip(spread, (2, 1, X - 1))]
    kept, rest, on_left, on_right = lax.optimization_barrier((kept, rest, on_left, on_right))
    (turned,) = local(
        turn_kernel, [((CUT, width), BF16)], kept, next_left, on_left, cost=AFTER_STARTS, name="turn"
    )
    mine_got = swap(turned, "head", 1)
    (below,) = local(
        below_kernel,
        [((CUT, width), BF16)],
        kept,
        on_right,
        next_right,
        mine_got,
        cost=AFTER_STARTS,
        name="below",
    )
    return local_out(last_kernel, ((rows, width), BF16), below, rest, *others)


def local_out(kernel, out, *ins):
    return pl.pallas_call(
        kernel,
        in_specs=[IN_VMEM] * len(ins),
        out_specs=IN_VMEM,
        out_shape=jax.ShapeDtypeStruct(*out),
        compiler_params=pltpu.CompilerParams(vmem_limit_bytes=VMEM_LIMIT),
        cost_estimate=LITTLE,
        name="last",
    )(*(held(a) for a in ins))


def solution(mesh):
    placed = (
        P("seq", "head"),
        P("seq", "head"),
        P("seq", "head"),
        P("seq", "head"),
        P("seq", "head"),
        P("head", None),
    )
    return jax.shard_map(
        body, mesh=mesh, in_specs=placed, out_specs=P("seq", "head"), check_vma=False
    )
```

```python
import functools
import math

import jax
import jax.numpy as jnp
from jax import lax
from jax.experimental import pallas as pl
from jax.experimental.pallas import tpu as pltpu
from jax.sharding import PartitionSpec as P

HD = 128
Z = 8
X = 4
BASE2 = math.log2(math.e) / math.sqrt(HD)
F32 = jnp.float32
BF16 = jnp.bfloat16
VMEM_LIMIT = 20 << 20
IN_VMEM = pl.BlockSpec(memory_space=pltpu.VMEM)
CUT = 256
LITTLE = pl.CostEstimate(flops=1, bytes_accessed=1, transcendentals=0)
AFTER_STARTS = pl.CostEstimate(flops=20_000_000_000, bytes_accessed=1, transcendentals=0)


def seq_place(i):
    return i // (2 * Z), (i // 2) % Z, i % 2


def between_frames():
    pairs = []
    for i in range(4 * Z):
        y, z, core = seq_place(i)
        other = (z + 1) % Z if z % 2 else (z - 1) % Z
        pairs.append((i, (y * Z + other) * 2 + core))
    return pairs


def between_frames_across():
    return [(i, to ^ 2 * Z) for i, to in between_frames()]


def along_x(step):
    return [(i, (i // 2 + step) % X * 2 + i % 2) for i in range(2 * X)]


def swap(value, axis, bit):
    return lax.ppermute(value, axis, [(i, i ^ bit) for i in range(lax.axis_size(axis))])


def held(array):
    return pltpu.with_memory_space_constraint(array, pltpu.VMEM)


def local(kernel, outs, *ins, scalars=(), scratch=(), cost=LITTLE, name="local"):
    return pl.pallas_call(
        kernel,
        in_specs=[pl.BlockSpec(memory_space=pltpu.SMEM)] * len(scalars) + [IN_VMEM] * len(ins),
        out_specs=[IN_VMEM] * len(outs),
        out_shape=[pltpu.VMEM(shape, dtype) for shape, dtype in outs],
        scratch_shapes=list(scratch),
        compiler_params=pltpu.CompilerParams(vmem_limit_bytes=VMEM_LIMIT),
        cost_estimate=cost,
        name=name,
    )(*scalars, *(held(a) for a in ins))


def stack_kernel(parts, n_ins, *refs):
    ins, outs, sems = refs[:n_ins], refs[n_ins:-1], refs[-1]
    copies = []
    for out, out_parts in zip(outs, parts):
        at = 0
        for place, low, high in out_parts:
            to = out.at[at : at + high - low, :]
            sem = sems.at[len(copies)]
            copies.append(pltpu.make_async_copy(ins[place].at[low:high, :], to, sem))
            at += high - low
    for copy in copies:
        copy.start()
    for copy in copies:
        copy.wait()


def stacked(arrays, parts=None, cost=LITTLE):
    parts = parts or (tuple((n, 0, a.shape[0]) for n, a in enumerate(arrays)),)
    width, dtype = arrays[0].shape[1], arrays[0].dtype
    return pl.pallas_call(
        functools.partial(stack_kernel, parts, len(arrays)),
        in_specs=[pl.BlockSpec(memory_space=pl.ANY)] * len(arrays),
        out_specs=[IN_VMEM] * len(parts),
        out_shape=[pltpu.VMEM((sum(h - l for _, l, h in part), width), dtype) for part in parts],
        scratch_shapes=[pltpu.SemaphoreType.DMA((sum(len(part) for part in parts),))],
        compiler_params=pltpu.CompilerParams(vmem_limit_bytes=VMEM_LIMIT),
        cost_estimate=cost,
        name="stacked",
    )(*arrays)


def scores_of(rows, keys):
    return lax.dot_general(rows, keys, (((1,), (1,)), ((), ())), preferred_element_type=F32)


def fill_keys(key_ref, value_ref, halves, pieces, columns):
    at = 0
    for half, piece in zip(halves, pieces):
        for low in range(0, piece.shape[0], 2 * half):
            key_ref[at : at + half, :] = piece[low : low + half, columns]
            value_ref[at : at + half, :HD] = piece[low + half : low + 2 * half, columns]
            at += half
    value_ref[:, HD:] = jnp.ones((at, HD), BF16)


def attend_kernel(halves, low, high, with_state, last, *refs):
    queries, refs = refs[:2], refs[2:]
    if with_state:
        (before, before_log), refs = refs[:2], refs[2:]
    pieces, refs = refs[: len(halves)], refs[len(halves) :]
    if last:
        (own_ref, own_log, other_ref, key_ref, value_ref, query_ref, log_ref) = refs
    else:
        (part_ref, log_ref, key_ref, value_ref, query_ref) = refs
    rows = high - low
    heads = queries[0].shape[1] // HD

    def scores_for(head):
        columns = slice(head * HD, (head + 1) * HD)
        slot = head % 2
        fill_keys(key_ref.at[slot], value_ref.at[slot], halves, pieces, columns)
        for place in range(2):
            query_ref[slot, place * rows : (place + 1) * rows, :] = queries[place][low:high, columns]
        return scores_of(query_ref[slot], key_ref[slot])

    next_scores = scores_for(0)
    for head in range(heads):
        columns = slice(head * HD, (head + 1) * HD)
        slot = head % 2
        scores = next_scores
        if head + 1 < heads:
            next_scores = scores_for(head + 1)
        peak = jnp.max(scores, axis=1, keepdims=True)
        weights = jnp.exp2((scores - peak) * BASE2).astype(BF16)
        both = jnp.dot(weights, value_ref[slot], preferred_element_type=F32)
        summed, total = both[:, :HD], both[:, HD:]
        peak = peak * BASE2
        for place in range(2):
            part = slice(place * rows, (place + 1) * rows)
            if with_state:
                log = before_log[part, head : head + 1]
                top = jnp.maximum(log, peak[part])
                before_factor = jnp.exp2(log - top)
                factor = jnp.exp2(peak[part] - top)
                whole = before_factor + total[part] * factor
                result = (before[part, columns] * before_factor + summed[part] * factor) / whole
            else:
                top = peak[part]
                whole = total[part]
                result = summed[part] / whole
            if last:
                (own_ref, other_ref)[place][:, columns] = result.astype(BF16)
            else:
                part_ref[part, columns] = result
            log_ref[part, head : head + 1] = (top + jnp.log2(whole))[:, :1]
    if last:
        lane = lax.broadcasted_iota(jnp.int32, (rows, HD), 1)
        own_log[...] = log_ref[:rows, :]
        logs = log_ref[rows:, :]
        high_part = logs.astype(BF16).astype(F32)
        rest = logs - high_part
        middle = rest.astype(BF16).astype(F32)
        packed = jnp.where(
            lane < 8,
            high_part,
            jnp.where(lane < 16, pltpu.roll(middle, 8, 1), pltpu.roll(rest - middle, 16, 1)),
        )
        other_ref[:, heads * HD :] = jnp.where(lane < 24, packed, 0.0).astype(BF16)


def attend(queries, other_queries, low, high, halves, pieces, state=None, last=False):
    whole_rows, width = queries.shape
    heads = width // HD
    rows = high - low
    keys = sum(piece.shape[0] for piece in pieces) // 2
    if last:
        outs = [((rows, width), BF16), ((rows, HD), F32), ((rows, width + HD), BF16)]
    else:
        outs = [((2 * rows, width), F32), ((2 * rows, HD), F32)]
    return local(
        functools.partial(attend_kernel, halves, low, high, state is not None, last),
        outs,
        queries,
        other_queries,
        *(state or ()),
        *pieces,
        scratch=[
            pltpu.VMEM((2, keys, HD), BF16),
            pltpu.VMEM((2, keys, 2 * HD), BF16),
            pltpu.VMEM((2, 2 * rows, HD), BF16),
        ]
        + [pltpu.VMEM((2 * rows, HD), F32)] * last,
        cost=LITTLE if last else AFTER_STARTS,
        name="attend_last" if last else "attend_part",
    )


def merge_heads(own, own_log, got, att):
    width = own.shape[1]
    logs = got[:, width:].astype(F32)
    got_log = logs + pltpu.roll(logs, HD - 8, 1) + pltpu.roll(logs, HD - 16, 1)
    for head in range(width // HD):
        columns = slice(head * HD, (head + 1) * HD)
        first, second = own_log[:, head : head + 1], got_log[:, head : head + 1]
        top = jnp.maximum(first, second)
        first_factor = jnp.exp2(first - top)
        second_factor = jnp.exp2(second - top)
        scale = 1.0 / (first_factor + second_factor)
        att[:, columns] = (
            own[:, columns].astype(F32) * (first_factor * scale)
            + got[:, columns].astype(F32) * (second_factor * scale)
        ).astype(BF16)


def products(blocks, place, att, weight, outs):
    rows, width = att.shape
    number = 0
    x, side = place[0] // 2, place[0] % 2
    for out in outs:
        for low in range(0, out.shape[0], rows):
            step, flip = blocks[number]
            block = lax.rem(x + step, X) * 2 + (1 - side if flip else side)
            at = pl.multiple_of(block * width, HD)
            result = jnp.dot(att[...], weight[:, pl.ds(at, width)], preferred_element_type=F32)
            out[low : low + rows, :] = result.astype(out.dtype)
            number += 1


def send_kernel(blocks, place, own, own_log, got, weight, *outs):
    merge_heads(own, own_log, got, outs[-1])
    products(blocks, place, outs[-1], weight, outs[:-1])


def project_send(blocks, place, own, own_log, got, weight, n_outs, cost=LITTLE):
    rows, width = own.shape
    count = len(blocks)
    outs = [((count // n_outs * rows, width), BF16)] * n_outs + [((rows, width), BF16)]
    return local(
        functools.partial(send_kernel, blocks),
        outs,
        own,
        own_log,
        got,
        weight,
        scalars=(place,),
        cost=cost,
        name="project_send",
    )


def keep_kernel(blocks, place, att, weight, *outs):
    products(blocks, place, att, weight, outs)


def project_keep(blocks, place, att, weight, n_outs=1, dtype=F32):
    rows, width = att.shape
    return local(
        functools.partial(keep_kernel, blocks),
        [((len(blocks) // n_outs * rows, width), dtype)] * n_outs,
        att,
        weight,
        scalars=(place,),
        name="project_keep",
    )


def relay_kernel(kept, got_left, got_right, to_right, to_left):
    n = got_left.shape[0]
    to_right[...] = (kept[:n, :] + got_left[...].astype(F32)).astype(BF16)
    to_left[...] = (kept[n : 2 * n, :] + got_right[...].astype(F32)).astype(BF16)


def turn_kernel(kept, next_left, on_left, out):
    n = out.shape[0]
    out[...] = (
        kept[3 * n :, :] + on_left[...].astype(F32) + next_left[...].astype(F32)
    ).astype(BF16)


def spread_kernel(kept, got, *outs):
    m = outs[0].shape[0]
    for number, out in enumerate(outs):
        rows = slice(number * m, (number + 1) * m)
        out[...] = (kept[rows, :] + got[rows, :].astype(F32)).astype(out.dtype)


def below_kernel(kept, on_right, next_right, mine, out):
    n = mine.shape[0]
    out[...] = (
        kept[2 * n : 3 * n, :]
        + on_right[...].astype(F32)
        + next_right[...].astype(F32)
        + mine[...].astype(F32)
    ).astype(BF16)


def last_kernel(below, rest, *refs):
    others, out = refs[:-1], refs[-1]
    n = below.shape[0]
    out[:n, :] = below[...]
    total = rest[...]
    for other in others:
        total = total + other[...].astype(F32)
    out[n:, :] = total.astype(BF16)


def body(queries, keys, values, ref_keys, ref_values, out_weight):
    rows, width = queries.shape
    half = ref_keys.shape[0]
    between = between_frames()
    right_x, left_x = along_x(1), along_x(-1)
    place = lax.axis_index("head").reshape(1)
    place, ref_keys = lax.optimization_barrier((place, ref_keys))
    keys, values, ref_keys, ref_values = (
        pltpu.with_memory_space_constraint(a, pltpu.HBM) for a in (keys, values, ref_keys, ref_values)
    )

    (own,) = stacked((ref_keys, ref_values))
    inner = [swap(own, "seq", 2)]
    outer = [lax.ppermute(own, "seq", between)]
    other_queries = swap(queries, "seq", 1)
    (keys, values), own = lax.optimization_barrier(((keys, values), own))
    parts = (rows // 4, rows // 4, rows // 2)
    lows = (0, rows // 4, rows // 2)
    frame = list(stacked(
        (keys, values),
        tuple(
            ((0, low, low + part), (1, low, low + part)) for low, part in zip(lows, parts)
        ),
    ))
    other_frame, across = [swap(frame[0], "seq", 2)], []
    for step in range(3):
        came_inner, came_outer = inner[-1], outer[-1]
        if step:
            came_inner, came_outer, other_frame[step - 1], other_queries = lax.optimization_barrier(
                (came_inner, came_outer, other_frame[step - 1], other_queries)
            )
        if step < 2:
            inner.append(swap(came_outer, "seq", 2))
        outer.append(lax.ppermute(came_inner, "seq", between))
        if step == 2:
            far_across = lax.ppermute(came_inner, "seq", between_frames_across())
        (packed,) = stacked([own] * (step == 0) + [came_inner, came_outer], cost=AFTER_STARTS)
        if step < 2:
            packed, frame[step + 1] = lax.optimization_barrier((packed, frame[step + 1]))
            other_frame.append(swap(frame[step + 1], "seq", 2))
        across.append(swap(packed, "seq", 2 * Z))

    early = (own, *inner[:2], *outer[:2], across[0])

    def attend_early(low, high):
        return attend(
            queries,
            other_queries,
            low,
            high,
            parts + parts[:2] + (half,) * len(early),
            (*frame, *other_frame[:2], *early),
        )

    state = attend_early(0, CUT)
    last_state = attend_early(CUT, rows)
    state, last_state = lax.optimization_barrier((state, last_state))
    pieces = (inner[2], *outer[2:], far_across, *across[1:], *other_frame[2:])
    halves = (half,) * (len(pieces) - 1) + parts[2:]

    def finish(low, high, state):
        own_part, own_log, other_part = attend(
            queries, other_queries, low, high, halves, pieces, state, True
        )
        return own_part, own_log, swap(other_part, "seq", 1)

    done = finish(0, CUT, state)
    go_right, go_left, att = project_send(((2, 0), (2, 1)), place, *done, out_weight, 2)

    last_done = finish(CUT, rows, last_state)
    last_done, go_right, go_left = lax.optimization_barrier((last_done, go_right, go_left))
    go_across, last_att = project_send(
        ((2, 1), (1, 1), (3, 1), (0, 1)), place, *last_done, out_weight, 1, AFTER_STARTS
    )
    got_across = swap(go_across, "head", 1)
    got_right = lax.ppermute(go_left, "head", left_x)
    got_left = lax.ppermute(go_right, "head", right_x)

    att, last_att = lax.optimization_barrier((att, last_att))
    next_go_right, next_go_left = project_keep(((1, 1), (3, 0)), place, att, out_weight, 2, BF16)
    next_left = lax.ppermute(next_go_right, "head", right_x)
    next_right = lax.ppermute(next_go_left, "head", left_x)
    att, next_go_right = lax.optimization_barrier((att, next_go_right))
    (kept,) = project_keep(((1, 0), (3, 1), (0, 0), (0, 1)), place, att, out_weight)

    one = ((CUT, width), BF16)
    to_right, to_left = local(relay_kernel, [one, one], kept, got_left, got_right, name="relay")
    on_right = lax.ppermute(to_right, "head", right_x)
    on_left = lax.ppermute(to_left, "head", left_x)

    last_att, next_left, next_right = lax.optimization_barrier((last_att, next_left, next_right))
    (last_kept,) = project_keep(
        ((2, 0), (1, 0), (3, 0), (0, 0)), place, last_att, out_weight
    )
    part = (rows - CUT, width)
    *spread, rest = local(
        spread_kernel, [(part, BF16)] * 3 + [(part, F32)], last_kept, got_across, name="spread"
    )
    sends = tuple(zip(spread, (2, 1, X - 1)))
    others = [lax.ppermute(a, "head", along_x(step)) for a, step in (*sends[1:], sends[0])]
    kept, rest, on_left, on_right = lax.optimization_barrier((kept, rest, on_left, on_right))
    (turned,) = local(
        turn_kernel, [((CUT, width), BF16)], kept, next_left, on_left, cost=AFTER_STARTS, name="turn"
    )
    mine_got = swap(turned, "head", 1)
    (below,) = local(
        below_kernel,
        [((CUT, width), BF16)],
        kept,
        on_right,
        next_right,
        mine_got,
        cost=AFTER_STARTS,
        name="below",
    )
    return local_out(last_kernel, ((rows, width), BF16), below, rest, *others)


def local_out(kernel, out, *ins):
    return pl.pallas_call(
        kernel,
        in_specs=[IN_VMEM] * len(ins),
        out_specs=IN_VMEM,
        out_shape=jax.ShapeDtypeStruct(*out),
        compiler_params=pltpu.CompilerParams(vmem_limit_bytes=VMEM_LIMIT),
        cost_estimate=LITTLE,
        name="last",
    )(*(held(a) for a in ins))


def solution(mesh):
    placed = (
        P("seq", "head"),
        P("seq", "head"),
        P("seq", "head"),
        P("seq", "head"),
        P("seq", "head"),
        P("head", None),
    )
    return jax.shard_map(
        body, mesh=mesh, in_specs=placed, out_specs=P("seq", "head"), check_vma=False
    )
```
